256 devices in a mesh: occ: 64 (over z, x, y_lo), aux: 4 (over y_hi, core).
Axes of the slice: x: 4, y: 4 (y_hi: 2, y_lo: 2; y = y_hi * 2 + y_lo), z: 8, core: 2. Of those that a mesh axis runs over, the one named last changes fastest.
Arguments:
- three_centre: float32 [16384, 24576], P('aux', 'occ'), may hold values from -0.625 to 0.625
- occ_energy: float32 [1536], P('occ'), may hold values from -1.5 to -0.3
- virt_energy: float32 [16], replicated, may hold values from 0.1 to 2
- pair_kept: int32 [2, 64], P(None, 'occ'), may hold values 0 or 1
Outputs:
- aux_gamma: float32 [16384, 24576], P('aux', 'occ')
The draws below stay inside these ranges and needn't reach their ends.
Inputs may be any that keep to these rules, and one draw needn't show every extreme that they name: pair_kept[s, K] is 1 where the pair of occupied blocks K and K - s - 1 (cyclic) is kept and 0 where it is screened out.
All inputs are finite; a program needn't handle non-finite values.
Results may differ from the reference program's by a relative error of at most 0.0003.
Values sent between devices are 32-bit elements; how exact they have to be, the bound alone decides.
A program may use at most 128 MiB of HBM per device.

```python
import jax
import jax.numpy as jnp
from jax import lax

NAUX = 16384
OCC_DEV = 24
VB = 16
STEPS = 2
NOCC = 1536
N_OCC = 64


def set_ends(values, stream_key, low, high):
    longest = values.shape.index(max(values.shape))
    spots = []
    for shift in (0, 1):
        where = [jax.random.randint(jax.random.fold_in(stream_key, axis), (), 0, length) for axis, length in enumerate(values.shape)]
        where[longest] = (where[longest] + shift) % values.shape[longest]
        spots.append(tuple(where))
    return values.at[spots[0]].set(low).at[spots[1]].set(high)


def shard_levels(own_key, extent, cuts, low, top_value):
    factor_of = 1.0
    for position, parts in cuts:
        steps = jax.random.uniform(jax.random.fold_in(jax.random.fold_in(own_key, 6), position), (parts,), jnp.float32, low / len(cuts), top_value / len(cuts))
        factor_of = factor_of * jnp.repeat(jnp.exp(steps), extent[position] // parts).reshape((-1,) + (1,) * (len(extent) - 1 - position))
    return factor_of


def noise(own_key, extent, deviation, bound, shards=(), held_as=jnp.bfloat16):
    drawn = jax.random.normal(own_key, extent, jnp.float32) * deviation
    if len(shards) > 0:
        drawn = shard_levels(own_key, extent, shards, -0.22, 0.18) * drawn
    return jnp.clip(drawn, min=-bound, max=bound).astype(held_as)


def setup_inputs(seed: int = 0) -> dict:
    splits = jax.random.split(jax.random.key(seed), 5)
    three_centre = noise(splits[0], (NAUX, NOCC * VB), 0.1, 0.625, ((0, 4), (1, 64)), jnp.float32)
    occ_energy = jnp.clip(-1.5 + 1.2 * jax.random.uniform(splits[1], (NOCC,), jnp.float32) ** shard_levels(splits[1], (NOCC,), ((0, 64),), -0.2, 0.2), -1.5, -0.3)
    virt_energy = jnp.clip(jax.random.uniform(splits[2], (VB,), jnp.float32, 0.1, 2.0), 0.1, 2.0)
    pair_kept = set_ends((jax.random.randint(splits[3], (STEPS, N_OCC), 0, 4) < 3).astype(jnp.int32), jax.random.fold_in(splits[3], 1), 0, 1)
    return dict(three_centre=three_centre, occ_energy=occ_energy, virt_energy=virt_energy, pair_kept=pair_kept)


exact_mode = lax.Precision.HIGHEST


def contract_rows(left_side, right_side):
    return lax.dot_general(left_side, right_side, (((0,), (0,)), ((), ())), precision=exact_mode, preferred_element_type=jnp.float32)


def times_transposed(left_side, right_side):
    return lax.dot_general(left_side, right_side, (((1,), (1,)), ((), ())), precision=exact_mode, preferred_element_type=jnp.float32)


def product(left_side, right_side):
    return jnp.dot(left_side, right_side, precision=exact_mode, preferred_element_type=jnp.float32)


def swap_virtuals(pair_block, virt_count):
    row_occ = pair_block.shape[0] // virt_count
    col_occ = pair_block.shape[1] // virt_count
    shaped = pair_block.reshape(row_occ, virt_count, col_occ, virt_count)
    return jnp.transpose(shaped, (0, 3, 2, 1)).reshape(pair_block.shape)


def denominators(row_levels, col_levels, virt_energy):
    virt_count = virt_energy.shape[0]
    occ_part = row_levels[:, None] + col_levels[None, :]
    virt_pairs = virt_energy[:, None] + virt_energy[None, :]
    spread_out = occ_part[:, None, :, None] - virt_pairs[None, :, None, :]
    return spread_out.reshape(row_levels.shape[0] * virt_count, col_levels.shape[0] * virt_count)


def amplitudes(pair_block, row_levels, col_levels, virt_energy, kept_flag):
    virt_count = virt_energy.shape[0]
    mixed_pairs = 2.0 * pair_block - swap_virtuals(pair_block, virt_count)
    return kept_flag * mixed_pairs / denominators(row_levels, col_levels, virt_energy)


def reference(three_centre, occ_energy, virt_energy, pair_kept):
    blocks = NOCC // OCC_DEV
    columns = OCC_DEV * VB
    tensor = three_centre.reshape(NAUX, blocks, columns)
    occ_levels = occ_energy.reshape(blocks, OCC_DEV)
    kept_table = pair_kept.astype(jnp.float32)

    def visit(density, block_index):
        own_block = lax.dynamic_index_in_dim(tensor, block_index, 1, keepdims=False)
        own_levels = lax.dynamic_index_in_dim(occ_levels, block_index, 0, keepdims=False)
        for cycle_step in range(STEPS):
            distance = cycle_step + 1
            other_block = ((block_index - distance) % blocks).astype(jnp.int32)
            partner = lax.dynamic_index_in_dim(tensor, other_block, 1, keepdims=False)
            partner_levels = lax.dynamic_index_in_dim(occ_levels, other_block, 0, keepdims=False)
            kept_flag = lax.dynamic_index_in_dim(kept_table[cycle_step], block_index, 0, keepdims=False)
            pair_block = contract_rows(own_block, partner)
            amplitude = amplitudes(pair_block, own_levels, partner_levels, virt_energy, kept_flag)
            density = density.at[:, block_index].add(times_transposed(partner, amplitude))
            density = density.at[:, other_block].add(product(own_block, amplitude))
        return density, None

    initial = jnp.zeros((NAUX, blocks, columns), jnp.float32)
    density = lax.scan(visit, initial, jnp.arange(blocks, dtype=jnp.int32))[0]
    return density.reshape(NAUX, blocks * columns)
```

```python
import functools

import jax
import jax.numpy as jnp
from jax import lax
from jax.experimental import pallas as pl
from jax.experimental.pallas import tpu as pltpu
from jax.sharding import PartitionSpec as P

MESH = pl.DeviceIdType.MESH
PAIRS = ((2, 0, 2), (2, 1, 1), (3, 1, 2), (3, 2, 1), (4, 2, 2), (4, 3, 1), (5, 3, 2))
C00, C01, C11, INTRA, N00, N01, N11 = range(7)
WINDOW = 2


def split(x):
    high = x.astype(jnp.bfloat16)
    return high, (x - high.astype(jnp.float32)).astype(jnp.bfloat16)


def dot3(a, b, dims):
    def one(x, y):
        return lax.dot_general(x, y, (dims, ((), ())), preferred_element_type=jnp.float32)

    return one(a[0], b[0]) + one(a[0], b[1]) + one(a[1], b[0])


ROWS = ((0,), (0,))
PLAIN = ((1,), (0,))
TURNED = ((1,), (1,))


def swap_virtuals(x, virt):
    rows, lanes = x.shape
    row = lax.broadcasted_iota(jnp.int32, x.shape, 0)
    lane = lax.broadcasted_iota(jnp.int32, x.shape, 1)
    step = 1
    while step < virt:
        row_bit, lane_bit = (row & step) != 0, (lane & step) != 0
        from_above = pltpu.roll(pltpu.roll(x, step, 0), lanes - step, 1)
        from_below = pltpu.roll(pltpu.roll(x, rows - step, 0), step, 1)
        moved = jnp.where(row_bit, from_above, from_below)
        x = jnp.where(row_bit == lane_bit, x, moved)
        step *= 2
    return x


def kernel(
    n_occ, virt,
    info_ref, b_ref, out_ref,
    w, pn, whi, wlo, phi, plo, s, ra, rb1, rb2, rx, ag, thi, tlo, ihi, ilo, rbuf, infos,
    info_s, info_r, y_s, y_r, x_s, x_r, l_s, st_s, st_r, c3_s, c3_r, r_s, r_r, o_s, o_r, lo_s,
):
    rows, cols = b_ref.shape
    half, quarter = rows // 2, rows // 4
    chunk = whi.shape[0] // 8
    count = quarter // chunk
    piece = cols // 8

    o, a = lax.axis_index("occ"), lax.axis_index("aux")
    yl, c, yh = lax.rem(o, 2), lax.rem(a, 2), lax.div(a, 2)
    ol, m2 = 1 - yl, o - lax.rem(o, 2)
    up, down = lax.rem(m2 + 2, n_occ), lax.rem(m2 + n_occ - 2, n_occ)
    y0, y1, y2, y3 = 2 * yh + yl, 2 * yh + ol, 2 * (1 - yh) + yl, 2 * (1 - yh) + ol
    partner, core = (m2 + ol, a), (o, a + 1 - 2 * c)
    across = (m2 + ol, 2 * (1 - yh) + c)
    prev, nxt = (down + yl, a), (up + yl, a)
    prev_x, nxt_x = (down + ol, a), (up + ol, a)
    onward, back = (nxt, prev), (prev, nxt)

    barrier = pltpu.get_barrier_semaphore()
    everyone = (partner, core, across, prev, nxt, prev_x, nxt_x)
    for device in everyone:
        pl.semaphore_signal(barrier, inc=1, device_id=device, device_id_type=MESH)
    pl.semaphore_wait(barrier, len(everyone))

    def remote(src, dst, ss, rs, device):
        return pltpu.make_async_remote_copy(
            src_ref=src, dst_ref=dst, send_sem=ss, recv_sem=rs, device_id=device, device_id_type=MESH
        )

    def landed(dst, rs):
        remote(dst, dst, rs, rs, partner).wait_recv()

    own = pltpu.make_async_copy(b_ref.at[pl.ds(yl * half, half)], w.at[yl], l_s.at[0])
    own.start()

    def at(h, k):
        return pl.ds(pl.multiple_of(h * quarter + k * chunk, chunk), chunk)

    def in_quarter(k):
        return pl.ds(pl.multiple_of(k * chunk, chunk), chunk)

    def y_copy(h, k):
        source = b_ref.at[pl.ds(pl.multiple_of(ol * half + h * quarter + k * chunk, chunk), chunk)]
        return remote(source, w.at[yl, at(h, k)], y_s.at[h, k], y_r.at[h, k], partner)

    def x_own(h, k):
        source = b_ref.at[pl.ds(pl.multiple_of(yl * half + h * quarter + k * chunk, chunk), chunk)]
        return remote(source, pn.at[h, yl, in_quarter(k)], x_s.at[0, h, k], x_r.at[0, h, k], onward[h])

    def x_relay(h, k):
        return remote(w.at[ol, at(h, k)], pn.at[h, ol, in_quarter(k)], x_s.at[1, h, k], x_r.at[1, h, k], onward[h])

    def start_y(k, _):
        for h in (0, 1):
            y_copy(h, k).start()
        return 0

    def start_x(k, _):
        for h in (0, 1):
            x_own(h, k).start()
        return 0

    lax.fori_loop(0, WINDOW, start_y, 0)
    lax.fori_loop(0, count, start_x, 0)

    mine = 2 + yl
    info_to = ((partner, 2 + yl), (nxt, yl), (nxt_x, yl), (prev, 4 + yl), (prev_x, 4 + yl))
    info_copies = [
        remote(info_ref, infos.at[slot], info_s.at[i], info_r.at[slot], device)
        for i, (device, slot) in enumerate(info_to)
    ]
    for copy in info_copies:
        copy.start()
    infos[mine] = info_ref[...]

    def clear(i, _):
        s[:, :, :, i] = jnp.zeros(s.shape[:3] + s.shape[4:], jnp.float32)
        return 0

    lax.fori_loop(0, 7, clear, 0)
    own.wait()

    def add_pair(index, value):
        s[:, :, :, index] += value.reshape(2, 4, 2, piece // 2, cols)

    even, odd = pl.ds(0, cols), pl.ds(cols, cols)

    def fetch(k, _):
        @pl.when(k < count)
        def _():
            for h in (0, 1):
                landed(w.at[ol, at(h, k)], y_r.at[h, k])
                x_relay(h, k).start()

                @pl.when(k + WINDOW < count)
                def _():
                    y_copy(h, k).wait_send()
                    y_copy(h, k + WINDOW).start()

                for parity, lanes in enumerate((even, odd)):
                    whi[at(h, k), lanes], wlo[at(h, k), lanes] = split(w[parity, at(h, k)])

        @pl.when(k > 0)
        def _():
            j = k - 1
            for h in (0, 1):
                landed(pn.at[h, yl, in_quarter(j)], x_r.at[0, h, j])
                landed(pn.at[h, ol, in_quarter(j)], x_r.at[1, h, j])
                for parity, lanes in enumerate((even, odd)):
                    phi[h, in_quarter(j), lanes], plo[h, in_quarter(j), lanes] = split(pn[h, parity, in_quarter(j)])
            w0 = whi[at(0, j), even], wlo[at(0, j), even]
            w1 = whi[at(0, j), odd], wlo[at(0, j), odd]
            both = phi[0, in_quarter(j)], plo[0, in_quarter(j)]
            mixed = tuple(jnp.concatenate([x, y[:, cols:]], axis=1) for x, y in zip(w0, both))
            found = dot3(w0, both, ROWS)
            add_pair(C00, found[:, :cols])
            add_pair(C01, found[:, cols:])
            found = dot3(w1, mixed, ROWS)
            add_pair(INTRA, found[:, :cols])
            add_pair(C11, found[:, cols:])
            both = whi[at(1, j)], wlo[at(1, j)]
            w0, w1 = tuple(x[:, :cols] for x in both), tuple(x[:, cols:] for x in both)
            n0 = phi[1, in_quarter(j), even], plo[1, in_quarter(j), even]
            n1 = phi[1, in_quarter(j), odd], plo[1, in_quarter(j), odd]
            found = dot3(n0, both, ROWS)
            add_pair(N00, found[:, :cols])
            add_pair(N01, found[:, cols:])
            add_pair(N11, dot3(n1, w1, ROWS))
            add_pair(INTRA, dot3(w1, w0, ROWS))

        return 0

    lax.fori_loop(0, count + 1, fetch, 0)

    step = remote(s.at[1 - c], ra, st_s.at[0], st_r.at[0], core)
    step.start()
    step.wait()

    def add_core(i, _):
        for h in (0, 1):
            s[c, i, h] += ra[i, h]
        return 0

    lax.fori_loop(0, 4, add_core, 0)
    steps = [
        remote(s.at[c, y1, 0], rb1.at[0, 0], st_s.at[1], st_r.at[1], partner),
        remote(s.at[c, y2, 0], rb1.at[0, 1], st_s.at[2], st_r.at[2], partner),
        remote(s.at[c, y3, 1], rb1.at[1, 0], st_s.at[3], st_r.at[3], across),
        remote(s.at[c, y2, 1], rb1.at[1, 1], st_s.at[4], st_r.at[4], across),
    ]
    for step in steps:
        step.start()
    for step in steps:
        step.wait()
    s[c, y3, 0] += rb1[0, 1]
    s[c, y1, 1] += rb1[1, 1]
    steps = [
        remote(s.at[c, y3, 0], rb2.at[0], st_s.at[5], st_r.at[5], across),
        remote(s.at[c, y1, 1], rb2.at[1], st_s.at[6], st_r.at[6], partner),
    ]
    for step in steps:
        step.start()
    for h in (0, 1):
        s[c, y0, h] += rb1[h, 0]
    for step in steps:
        step.wait()
    for h in (0, 1):
        s[c, y0, h] += rb2[h]
    steps = [
        remote(s.at[c, y0, :, pl.ds(0, 3)], rx.at[1], st_s.at[7], st_r.at[7], prev),
        remote(s.at[c, y0, :, pl.ds(4, 3)], rx.at[0], st_s.at[8], st_r.at[8], nxt),
    ]
    for step in steps:
        step.start()

    for slot in (0, 1, 2 + ol, 4, 5):
        landed(infos.at[slot], info_r.at[slot])
    first = (c * 4 + y0) * piece
    row = lax.broadcasted_iota(jnp.int32, (piece, cols), 0)
    lane = lax.broadcasted_iota(jnp.int32, (piece, cols), 1)
    levels = {
        slot: jnp.sum(jnp.where(lane == row + first, infos[slot, pl.ds(0, 1)], 0.0), axis=1, keepdims=True)
        for slot in (2, 3, 4, 5)
    }

    def amplitude(index):
        k_slot, l_slot, distance = PAIRS[index]
        block = s[c, y0, :, index]
        if index < 3:
            block = block + rx[0, :, index]
        elif index > 3:
            block = block + rx[1, :, index - 4]
        block = block.reshape(piece, cols)
        swapped = jnp.concatenate(
            [swap_virtuals(block[:, i : i + 128], virt) for i in range(0, cols, 128)], axis=1
        )
        gap = levels[k_slot] + infos[l_slot, pl.ds(0, 1)]
        result = infos[k_slot, pl.ds(distance, 1)] * (2.0 * block - swapped) / gap
        ag[c, y0, :, index] = result.reshape(2, piece // 2, cols)

    amplitude(INTRA)
    for step in steps:
        step.wait()
    for index in (C00, C01, C11, N00, N01, N11):
        amplitude(index)

    def y_part(owner, h, device, i):
        return remote(ag.at[c, owner, h], ag.at[c, owner, h], st_s.at[i], st_r.at[i], device)

    def core_part(owner, h):
        return remote(ag.at[c, owner, h], ag.at[c, owner, h], c3_s.at[owner, h], c3_r.at[owner, h], core)

    first_steps = [
        y_part(y0, 0, across, 9), y_part(y0, 1, partner, 10), y_part(y0, 0, partner, 11), y_part(y0, 1, across, 12),
    ]
    for step in first_steps:
        step.start()
    for h in (0, 1):
        core_part(y0, h).start()
    landed(ag.at[c, y3, 0], st_r.at[9])
    second_steps = [y_part(y3, 0, partner, 13)]
    second_steps[0].start()
    core_part(y3, 0).start()
    landed(ag.at[c, y1, 1], st_r.at[10])
    second_steps.append(y_part(y1, 1, across, 14))
    second_steps[1].start()
    core_part(y1, 1).start()
    for owner, h, i in ((y1, 0, 11), (y3, 1, 12), (y2, 0, 13), (y2, 1, 14)):
        landed(ag.at[c, owner, h], st_r.at[i])
        core_part(owner, h).start()

    def sent(k, _):
        for h in (0, 1):
            x_own(h, k).wait_send()
            x_relay(h, k).wait_send()

            @pl.when(k >= count - WINDOW)
            def _():
                y_copy(h, k).wait_send()

        return 0

    lax.fori_loop(0, count, sent, 0)
    for copy in info_copies:
        copy.wait_send()
    for step in first_steps + second_steps:
        step.wait_send()

    zero = jnp.zeros((cols, cols), jnp.bfloat16)
    for i in (0, 1):
        thi[i, odd, even] = zero
        tlo[i, odd, even] = zero

    def core_landed(i, _):
        for h in (0, 1):
            core_part(i, h).wait_send()
            landed(ag.at[1 - c, i, h], c3_r.at[i, h])
        return 0

    lax.fori_loop(0, 4, core_landed, 0)

    def whole(index):
        return split(ag[:, :, :, index].reshape(cols, cols))

    for i, indices in enumerate(((C00, C01, C11), (N00, N01, N11))):
        for index, (top, left) in zip(indices, ((even, even), (even, odd), (odd, odd))):
            thi[i, top, left], tlo[i, top, left] = whole(index)
    ihi[...], ilo[...] = whole(INTRA)

    def r_copy(far, h, k):
        parity = ol if far else yl
        place = (h, parity, in_quarter(k))
        i = 0 if far else 1
        return remote(rbuf.at[place], pn.at[place], r_s.at[i, h, k], r_r.at[i, h, k], back[h])

    def give(k, _):
        for h in (0, 1):
            left = whi[at(h, k)], wlo[at(h, k)]
            found = dot3(left, (thi[h], tlo[h]), TURNED if h else PLAIN)
            rbuf[h, 0, in_quarter(k)] = found[:, :cols]
            rbuf[h, 1, in_quarter(k)] = found[:, cols:]
            r_copy(True, h, k).start()
            r_copy(False, h, k).start()
        return 0

    lax.fori_loop(0, count, give, 0)

    def o_copy(h, k):
        target = out_ref.at[pl.ds(pl.multiple_of(yl * half + h * quarter + k * chunk, chunk), chunk)]
        return remote(w.at[ol, at(h, k)], target, o_s.at[h, k], o_r.at[h, k], partner)

    def keep(h, k):
        target = out_ref.at[pl.ds(pl.multiple_of(yl * half + h * quarter + k * chunk, chunk), chunk)]
        return pltpu.make_async_copy(w.at[yl, at(h, k)], target, lo_s.at[h, k])

    def gather(k, _):
        for h in (0, 1):
            found = dot3((phi[h, in_quarter(k)], plo[h, in_quarter(k)]), (thi[h], tlo[h]), PLAIN if h else TURNED)
            inner = ihi[...], ilo[...]
            w0 = whi[at(h, k), even], wlo[at(h, k), even]
            w1 = whi[at(h, k), odd], wlo[at(h, k), odd]
            w[0, at(h, k)] = found[:, :cols] + dot3(w1, inner, PLAIN)
            w[1, at(h, k)] = found[:, cols:] + dot3(w0, inner, TURNED)
            landed(pn.at[h, ol, in_quarter(k)], r_r.at[0, h, k])
            w[ol, at(h, k)] += pn[h, ol, in_quarter(k)]
            o_copy(h, k).start()
            landed(pn.at[h, yl, in_quarter(k)], r_r.at[1, h, k])
            w[yl, at(h, k)] += pn[h, yl, in_quarter(k)]
            keep(h, k).start()
        return 0

    lax.fori_loop(0, count, gather, 0)

    def finish(k, _):
        for h in (0, 1):
            r_copy(True, h, k).wait_send()
            r_copy(False, h, k).wait_send()
            keep(h, k).wait()
            o_copy(h, k).wait_send()
            theirs = pl.ds(pl.multiple_of(ol * half + h * quarter + k * chunk, chunk), chunk)
            landed(out_ref.at[theirs], o_r.at[h, k])
        return 0

    lax.fori_loop(0, count, finish, 0)


def solution(mesh):
    n_occ = mesh.shape["occ"]

    def shards(three_centre, occ_energy, virt_energy, pair_kept):
        rows, cols = three_centre.shape
        occ, virt = occ_energy.shape[0], virt_energy.shape[0]
        levels = (occ_energy[:, None] - virt_energy[None, :]).reshape(1, cols)
        kept = jnp.broadcast_to(pair_kept.astype(jnp.float32), (pair_kept.shape[0], cols))
        info = jnp.concatenate([levels, kept, jnp.zeros((8 - 1 - kept.shape[0], cols), jnp.float32)], axis=0)
        half, quarter = rows // 2, rows // 4
        chunk = rows // 16
        count = quarter // chunk
        part = (7, cols // 16, cols)
        f32, bf16 = jnp.float32, jnp.bfloat16
        dma = pltpu.SemaphoreType.DMA
        return pl.pallas_call(
            functools.partial(kernel, n_occ, virt),
            out_shape=jax.ShapeDtypeStruct((rows, cols), f32),
            in_specs=[pl.BlockSpec(memory_space=pltpu.VMEM), pl.BlockSpec(memory_space=pl.ANY)],
            out_specs=pl.BlockSpec(memory_space=pl.ANY),
            scratch_shapes=[
                pltpu.VMEM((2, half, cols), f32),
                pltpu.VMEM((2, 2, quarter, cols), f32),
                pltpu.VMEM((half, 2 * cols), bf16),
                pltpu.VMEM((half, 2 * cols), bf16),
                pltpu.VMEM((2, quarter, 2 * cols), bf16),
                pltpu.VMEM((2, quarter, 2 * cols), bf16),
                pltpu.VMEM((2, 4, 2) + part, f32),
                pltpu.VMEM((4, 2) + part, f32),
                pltpu.VMEM((2, 2) + part, f32),
                pltpu.VMEM((2,) + part, f32),
                pltpu.VMEM((2, 2, 3) + part[1:], f32),
                pltpu.VMEM((2, 4, 2) + part, f32),
                pltpu.VMEM((2, 2 * cols, 2 * cols), bf16),
                pltpu.VMEM((2, 2 * cols, 2 * cols), bf16),
                pltpu.VMEM((cols, cols), bf16),
                pltpu.VMEM((cols, cols), bf16),
                pltpu.VMEM((2, 2, quarter, cols), f32),
                pltpu.VMEM((6, 8, cols), f32),
                dma((5,)), dma((6,)),
                dma((2, count)), dma((2, count)),
                dma((2, 2, count)), dma((2, 2, count)),
                dma((1,)),
                dma((15,)), dma((15,)),
                dma((4, 2)), dma((4, 2)),
                dma((2, 2, count)), dma((2, 2, count)),
                dma((2, count)), dma((2, count)), dma((2, count)),
            ],
            compiler_params=pltpu.CompilerParams(
                collective_id=0, has_side_effects=True, vmem_limit_bytes=60 * 2**20
            ),
        )(info, three_centre)

    return jax.shard_map(
        shards,
        mesh=mesh,
        in_specs=(P("aux", "occ"), P("occ"), P(), P(None, "occ")),
        out_specs=P("aux", "occ"),
        check_vma=False,
    )
```

```python
import functools

import jax
import jax.numpy as jnp
from jax import lax
from jax.experimental import pallas as pl
from jax.experimental.pallas import tpu as pltpu
from jax.sharding import PartitionSpec as P

MESH = pl.DeviceIdType.MESH
OWN, Y, T, OWN_D, D = range(5)
WINDOW = 2
LAG = 2


def split(x):
    high = x.astype(jnp.bfloat16)
    return high, (x - high.astype(jnp.float32)).astype(jnp.bfloat16)


def dot3(a, b, dims):
    def one(x, y):
        return lax.dot_general(x, y, (dims, ((), ())), preferred_element_type=jnp.float32)

    return one(a[0], b[0]) + one(a[0], b[1]) + one(a[1], b[0])


ROWS = ((0,), (0,))
PLAIN = ((1,), (0,))
TURNED = ((1,), (1,))


def beside(a, b):
    return tuple(jnp.concatenate([x, y], axis=1) for x, y in zip(a, b))


def swap_virtuals(x, virt):
    rows, lanes = x.shape
    row = lax.broadcasted_iota(jnp.int32, x.shape, 0)
    lane = lax.broadcasted_iota(jnp.int32, x.shape, 1)
    step = 1
    while step < virt:
        row_bit, lane_bit = (row & step) != 0, (lane & step) != 0
        from_above = pltpu.roll(pltpu.roll(x, step, 0), lanes - step, 1)
        from_below = pltpu.roll(pltpu.roll(x, rows - step, 0), step, 1)
        moved = jnp.where(row_bit, from_above, from_below)
        x = jnp.where(row_bit == lane_bit, x, moved)
        step *= 2
    return x


def kernel(
    n_occ, chunk,
    occ_ref, virt_ref, kept_ref, b_ref, out_ref,
    z, zhi, zlo, s, ra, rb, ag, mdh, mdl, mah, mal, mbh, mbl, rbuf, infos,
    info_s, info_r, f_s, f_r, l_s, a_s, a_r, b_s, b_r, g_s, g_r, c_s, c_r, r_s, r_r, o_s,
):
    rows, cols = b_ref.shape
    half = rows // 2
    count = half // chunk
    piece = cols // 8
    occ, virt = occ_ref.shape[0], virt_ref.shape[0]

    o, a = lax.axis_index("occ"), lax.axis_index("aux")
    yl, c, yh = lax.rem(o, 2), lax.rem(a, 2), lax.div(a, 2)
    ol, m2 = 1 - yl, o - lax.rem(o, 2)
    up, down = lax.rem(m2 + 2, n_occ), lax.rem(m2 + n_occ - 2, n_occ)
    toward, away = ol * up + yl * down, ol * down + yl * up
    core = (o, a + 1 - 2 * c)
    here, there = a, 2 * (1 - yh) + c
    xd, xt, partner, diagonal = toward + yl, away + yl, m2 + ol, toward + ol
    others = (xt, xd, partner, diagonal)
    tile_there = (1, 0, 2, 3)
    site = (0, 1, yl, yl)

    barrier = pltpu.get_barrier_semaphore()
    everyone = [core, (o, there)] + [(x, y) for x in others for y in (here, there)]
    for device in everyone:
        pl.semaphore_signal(barrier, inc=1, device_id=device, device_id_type=MESH)
    pl.semaphore_wait(barrier, len(everyone))

    def remote(src, dst, ss, rs, device):
        return pltpu.make_async_remote_copy(
            src_ref=src, dst_ref=dst, send_sem=ss, recv_sem=rs, device_id=device, device_id_type=MESH
        )

    def landed(dst, rs):
        remote(dst, dst, rs, rs, (partner, a)).wait_recv()

    def place(k):
        return pl.ds(pl.multiple_of(k * chunk, chunk), chunk)

    def source(side, k):
        return pl.ds(pl.multiple_of(side * half + k * chunk, chunk), chunk)

    side_t, side_d = ol, yl

    def send_copies(k):
        return (
            remote(b_ref.at[source(side_d, k)], z.at[Y, place(k)], f_s.at[0, k], f_r.at[0, k], (partner, a)),
            remote(b_ref.at[source(side_t, k)], z.at[T, place(k)], f_s.at[1, k], f_r.at[1, k], (xt, a)),
            remote(b_ref.at[source(side_d, k)], z.at[D, place(k)], f_s.at[2, k], f_r.at[2, k], (xd, a)),
        )

    arrivals = (Y, T, D)
    for k in range(WINDOW):
        for copy in send_copies(k):
            copy.start()
    own = [
        pltpu.make_async_copy(b_ref.at[pl.ds(side_t * half, half)], z.at[OWN], l_s.at[0]),
        pltpu.make_async_copy(b_ref.at[pl.ds(side_d * half, half)], z.at[OWN_D], l_s.at[1]),
    ]
    for copy in own:
        copy.start()

    row = lax.broadcasted_iota(jnp.int32, (8, cols), 0)
    lane = lax.broadcasted_iota(jnp.int32, (8, cols), 1)
    levels = jnp.zeros((8, cols), jnp.float32)
    for i in range(occ):
        levels = jnp.where((lane >= i * virt) & (lane < (i + 1) * virt), occ_ref[i], levels)
    empty = jnp.zeros((8, cols), jnp.float32)
    for i in range(virt):
        empty = jnp.where((lane & (virt - 1)) == i, virt_ref[i], empty)
    kept = jnp.where(row == 1, kept_ref[0, 0].astype(jnp.float32), kept_ref[1, 0].astype(jnp.float32))
    infos[0] = jnp.where(row == 0, levels - empty, kept)
    info_copies = [
        remote(infos.at[0], infos.at[i], info_s.at[i - 1], info_r.at[i - 1], (device, a))
        for i, device in ((1, partner), (2, xt), (3, xd))
    ]
    for copy in info_copies:
        copy.start()

    def clear(i, _):
        s[i] = jnp.zeros(s.shape[1:], jnp.float32)
        return 0

    lax.fori_loop(0, 4, clear, 0)
    for copy in own:
        copy.wait()

    def add_pair(index, value):
        s[index] += value.reshape(2, 4, piece, cols)

    def held(block, k):
        return zhi[block, place(k)], zlo[block, place(k)]

    def divide(block, k):
        zhi[block, place(k)], zlo[block, place(k)] = split(z[block, place(k)])

    def fetch(k, _):
        divide(OWN, k)
        divide(OWN_D, k)
        for i, block in enumerate(arrivals):
            landed(z.at[block, place(k)], f_r.at[i, k])

        @pl.when(k + WINDOW < count)
        def _():
            for copy in send_copies(k):
                copy.wait_send()
            for copy in send_copies(k + WINDOW):
                copy.start()

        for block in arrivals:
            divide(block, k)
        found = dot3(held(2 - yl, k), beside(held(OWN, k), held(1 + yl, k)), ROWS)
        add_pair(1 + yl, found[:, :cols])
        add_pair(3, found[:, cols:])
        add_pair(2 - yl, dot3(held(2 * yl, k), held(1 - yl, k), ROWS))
        add_pair(0, dot3(held(OWN_D, k), held(D, k), ROWS))
        return 0

    lax.fori_loop(0, count, fetch, 0)

    order = (3, 2, 1, 0)
    step_a = {b: remote(s.at[b, 1 - c], ra.at[b], a_s.at[b], a_r.at[b], core) for b in order}
    for b in order:
        step_a[b].start()
    mine = [2 * site[b] + yh for b in range(4)]

    def members(b):
        far, across = 2 * site[b] + 1 - yh, 2 * (1 - site[b])
        return (
            ((o, there), far, b),
            ((others[b], here), across + yh, tile_there[b]),
            ((others[b], there), across + 1 - yh, tile_there[b]),
        )

    step_b = {
        b: [
            remote(s.at[b, c, q], rb.at[t, i], b_s.at[b, i], b_r.at[t, i], device)
            for i, (device, q, t) in enumerate(members(b))
        ]
        for b in order
    }
    for b in order:
        step_a[b].wait()
        s[b, c] += ra[b]
        for copy in step_b[b]:
            copy.start()

    for i in range(3):
        landed(infos.at[i + 1], info_r.at[i])
    row = lax.broadcasted_iota(jnp.int32, (piece, cols), 0)
    lane = lax.broadcasted_iota(jnp.int32, (piece, cols), 1)
    row_info, col_info = (0, 2, yl, 2 - yl), (3, 0, ol, 1 + yl)
    kept_info, distance = (3 * yl, 2 * ol, ol, 2 - yl), (2, 2, 1, 1)

    step_g = {
        b: [
            remote(ag.at[b, c, mine[b]], ag.at[t, c, mine[b]], g_s.at[b, i], g_r.at[t, i], device)
            for i, (device, q, t) in enumerate(members(b))
        ]
        for b in order
    }

    def core_copy(b, q):
        return remote(ag.at[b, c, q], ag.at[b, c, q], c_s.at[b, q], c_r.at[b, q], core)

    for b in order:
        first = (c * 4 + mine[b]) * piece
        level = jnp.sum(jnp.where(lane == row + first, infos[row_info[b], pl.ds(0, 1)], 0.0), axis=1, keepdims=True)
        gap = level + infos[col_info[b], pl.ds(0, 1)]
        for i in range(3):
            landed(rb.at[b, i], b_r.at[b, i])
        block = s[b, c, mine[b]] + rb[b, 0] + rb[b, 1] + rb[b, 2]
        swapped = jnp.concatenate([swap_virtuals(block[:, i : i + 128], virt) for i in range(0, cols, 128)], axis=1)
        ag[b, c, mine[b]] = infos[kept_info[b], pl.ds(distance[b], 1)] * (2.0 * block - swapped) / gap
        for copy in step_g[b]:
            copy.start()
        core_copy(b, mine[b]).start()

    def sent(k, _):
        for copy in send_copies(k):
            copy.wait_send()
        return 0

    lax.fori_loop(count - WINDOW, count, sent, 0)
    for copy in info_copies:
        copy.wait_send()
    for b in order:
        for i, (_, q, t) in enumerate(members(b)):
            landed(ag.at[b, c, q], g_r.at[b, i])
            core_copy(b, q).start()

    def whole(b):
        for q in range(4):
            landed(ag.at[b, 1 - c, q], c_r.at[b, q])
        return ag[b].reshape(cols, cols)

    left, right = pl.ds(0, cols), pl.ds(cols, cols)
    t_to_y, own_to_y = whole(3), whole(2)

    @pl.when(yl == 0)
    def _():
        mah[:, right], mal[:, right] = split(t_to_y)
        mbh[right, :], mbl[right, :] = split(t_to_y)
        mbh[left, :], mbl[left, :] = split(own_to_y)

    @pl.when(yl == 1)
    def _():
        turned = t_to_y.T
        mah[:, right], mal[:, right] = split(turned)
        mbh[right, :], mbl[right, :] = split(turned)
        mbh[left, :], mbl[left, :] = split(own_to_y.T)

    mah[:, left], mal[:, left] = split(whole(1))
    mdh[...], mdl[...] = split(whole(0))

    def give_copies(k):
        return (
            remote(rbuf.at[0, place(k)], z.at[Y, place(k)], r_s.at[0, k], r_r.at[0, k], (partner, a)),
            remote(rbuf.at[1, place(k)], z.at[T, place(k)], r_s.at[1, k], r_r.at[1, k], (xd, a)),
            remote(rbuf.at[2, place(k)], z.at[D, place(k)], r_s.at[2, k], r_r.at[2, k], (xt, a)),
        )

    def write_copies(k):
        return (
            pltpu.make_async_copy(z.at[OWN, place(k)], out_ref.at[source(side_t, k)], o_s.at[0, k]),
            pltpu.make_async_copy(z.at[OWN_D, place(k)], out_ref.at[source(side_d, k)], o_s.at[1, k]),
        )

    def finish(k, _):
        @pl.when(k < count)
        def _():
            @pl.when(k >= WINDOW)
            def _():
                for copy in give_copies(k - WINDOW):
                    copy.wait_send()

            own_t, y, t, own_d, d = (held(block, k) for block in range(5))
            rbuf[0, place(k)] = dot3(beside(own_t, t), (mbh[...], mbl[...]), PLAIN)
            rbuf[1, place(k)] = dot3(beside(own_t, y), (mah[...], mal[...]), TURNED)
            rbuf[2, place(k)] = dot3(own_d, (mdh[...], mdl[...]), PLAIN)
            for copy in give_copies(k):
                copy.start()
            z[OWN, place(k)] = dot3(t, (mah[:, left], mal[:, left]), PLAIN) + dot3(
                y, (mbh[left, :], mbl[left, :]), TURNED
            )
            z[OWN_D, place(k)] = dot3(d, (mdh[...], mdl[...]), TURNED)

        @pl.when(k >= LAG)
        def _():
            j = k - LAG
            for i, block in enumerate(arrivals):
                landed(z.at[block, place(j)], r_r.at[i, j])
            z[OWN, place(j)] += z[T, place(j)]
            z[OWN_D, place(j)] += z[Y, place(j)] + z[D, place(j)]
            for copy in write_copies(j):
                copy.start()

        return 0

    lax.fori_loop(0, count + LAG, finish, 0)

    def written(k, _):
        for copy in write_copies(k):
            copy.wait()
        return 0

    lax.fori_loop(0, count, written, 0)

    def given(k, _):
        for copy in give_copies(k):
            copy.wait_send()
        return 0

    lax.fori_loop(count - WINDOW, count, given, 0)
    for b in order:
        for copy in step_b[b] + step_g[b]:
            copy.wait_send()
        for q in range(4):
            core_copy(b, q).wait_send()


def solution(mesh):
    n_occ = mesh.shape["occ"]

    def shards(three_centre, occ_energy, virt_energy, pair_kept):
        rows, cols = three_centre.shape
        half, chunk = rows // 2, rows // 16
        count = half // chunk
        piece = (cols // 8, cols)
        f32, bf16 = jnp.float32, jnp.bfloat16
        dma = pltpu.SemaphoreType.DMA
        return pl.pallas_call(
            functools.partial(kernel, n_occ, chunk),
            out_shape=jax.ShapeDtypeStruct((rows, cols), f32),
            in_specs=[pl.BlockSpec(memory_space=pltpu.SMEM)] * 3 + [pl.BlockSpec(memory_space=pl.ANY)],
            out_specs=pl.BlockSpec(memory_space=pl.ANY),
            scratch_shapes=[
                pltpu.VMEM((5, half, cols), f32),
                pltpu.VMEM((5, half, cols), bf16),
                pltpu.VMEM((5, half, cols), bf16),
                pltpu.VMEM((4, 2, 4) + piece, f32),
                pltpu.VMEM((4, 4) + piece, f32),
                pltpu.VMEM((4, 3) + piece, f32),
                pltpu.VMEM((4, 2, 4) + piece, f32),
                pltpu.VMEM((cols, cols), bf16),
                pltpu.VMEM((cols, cols), bf16),
                pltpu.VMEM((cols, 2 * cols), bf16),
                pltpu.VMEM((cols, 2 * cols), bf16),
                pltpu.VMEM((2 * cols, cols), bf16),
                pltpu.VMEM((2 * cols, cols), bf16),
                pltpu.VMEM((3, half, cols), f32),
                pltpu.VMEM((4, 8, cols), f32),
                dma((3,)), dma((3,)),
                dma((3, count)), dma((3, count)), dma((2,)),
                dma((4,)), dma((4,)),
                dma((4, 3)), dma((4, 3)),
                dma((4, 3)), dma((4, 3)),
                dma((4, 4)), dma((4, 4)),
                dma((3, count)), dma((3, count)), dma((2, count)),
            ],
            compiler_params=pltpu.CompilerParams(
                collective_id=0, has_side_effects=True, vmem_limit_bytes=60 * 2**20
            ),
        )(occ_energy, virt_energy, pair_kept, three_centre)

    return jax.shard_map(
        shards,
        mesh=mesh,
        in_specs=(P("aux", "occ"), P("occ"), P(), P(None, "occ")),
        out_specs=P("aux", "occ"),
        check_vma=False,
    )
```

```python
import functools

import jax
import jax.numpy as jnp
from jax import lax
from jax.experimental import pallas as pl
from jax.experimental.pallas import tpu as pltpu
from jax.sharding import PartitionSpec as P

MESH = pl.DeviceIdType.MESH
Y, T, D, OWN, OWN_D = range(5)
WINDOW = 2
LAG = 2


def split(x):
    high = x.astype(jnp.bfloat16)
    return high, (x - high.astype(jnp.float32)).astype(jnp.bfloat16)


def dot3(a, b, dims):
    def one(x, y):
        return lax.dot_general(x, y, (dims, ((), ())), preferred_element_type=jnp.float32)

    return one(a[0], b[0]) + one(a[0], b[1]) + one(a[1], b[0])


ROWS = ((0,), (0,))
PLAIN = ((1,), (0,))
TURNED = ((1,), (1,))


def beside(a, b):
    return tuple(jnp.concatenate([x, y], axis=1) for x, y in zip(a, b))


def swap_virtuals(x, virt):
    rows, lanes = x.shape
    row = lax.broadcasted_iota(jnp.int32, x.shape, 0)
    lane = lax.broadcasted_iota(jnp.int32, x.shape, 1)
    step = 1
    while step < virt:
        row_bit, lane_bit = (row & step) != 0, (lane & step) != 0
        from_above = pltpu.roll(pltpu.roll(x, step, 0), lanes - step, 1)
        from_below = pltpu.roll(pltpu.roll(x, rows - step, 0), step, 1)
        moved = jnp.where(row_bit, from_above, from_below)
        x = jnp.where(row_bit == lane_bit, x, moved)
        step *= 2
    return x


def kernel(
    n_occ, chunk,
    occ_ref, virt_ref, kept_ref, b_ref, out_ref,
    z, zhi, zlo, s, ra, rb, ag, mdh, mdl, mah, mal, mbh, mbl, rbuf, infos,
    info_s, info_r, f_s, f_r, l_s, a_s, a_r, b_s, b_r, g_s, g_r, c_s, c_r, r_s, r_r,
):
    rows, cols = b_ref.shape
    half = rows // 2
    count = half // chunk
    piece = cols // 8
    occ, virt = occ_ref.shape[0], virt_ref.shape[0]

    o, a = lax.axis_index("occ"), lax.axis_index("aux")
    yl, c, yh = lax.rem(o, 2), lax.rem(a, 2), lax.div(a, 2)
    ol, m2 = 1 - yl, o - lax.rem(o, 2)
    up, down = lax.rem(m2 + 2, n_occ), lax.rem(m2 + n_occ - 2, n_occ)
    toward, away = ol * up + yl * down, ol * down + yl * up
    core = (o, a + 1 - 2 * c)
    here, there = a, 2 * (1 - yh) + c
    xd, xt, partner, diagonal = toward + yl, away + yl, m2 + ol, toward + ol
    others = (xt, xd, partner, diagonal)
    tile_there = (1, 0, 2, 3)
    site = (0, 1, yl, yl)

    barrier = pltpu.get_barrier_semaphore()
    everyone = [core, (o, there)] + [(x, y) for x in others for y in (here, there)]
    for device in everyone:
        pl.semaphore_signal(barrier, inc=1, device_id=device, device_id_type=MESH)
    pl.semaphore_wait(barrier, len(everyone))

    def remote(src, dst, ss, rs, device):
        return pltpu.make_async_remote_copy(
            src_ref=src, dst_ref=dst, send_sem=ss, recv_sem=rs, device_id=device, device_id_type=MESH
        )

    def landed(dst, rs):
        remote(dst, dst, rs, rs, (partner, a)).wait_recv()

    def place(k):
        return pl.ds(pl.multiple_of(k * chunk, chunk), chunk)

    def source(side, k):
        return pl.ds(pl.multiple_of(side * half + k * chunk, chunk), chunk)

    side_t, side_d = ol, yl

    def send_copies(k):
        return (
            remote(b_ref.at[source(side_d, k)], z.at[Y, place(k)], f_s.at[0, k], f_r.at[0, k], (partner, a)),
            remote(b_ref.at[source(side_t, k)], z.at[T, place(k)], f_s.at[1, k], f_r.at[1, k], (xt, a)),
            remote(b_ref.at[source(side_d, k)], z.at[D, place(k)], f_s.at[2, k], f_r.at[2, k], (xd, a)),
        )

    arrivals = (Y, T, D)
    for k in range(WINDOW):
        for copy in send_copies(k):
            copy.start()
    own = [
        pltpu.make_async_copy(b_ref.at[pl.ds(side_t * half, half)], out_ref.at[pl.ds(side_t * half, half)], l_s.at[0]),
        pltpu.make_async_copy(b_ref.at[pl.ds(side_d * half, half)], out_ref.at[pl.ds(side_d * half, half)], l_s.at[1]),
    ]
    for copy in own:
        copy.start()

    row = lax.broadcasted_iota(jnp.int32, (8, cols), 0)
    lane = lax.broadcasted_iota(jnp.int32, (8, cols), 1)
    levels = jnp.zeros((8, cols), jnp.float32)
    for i in range(occ):
        levels = jnp.where((lane >= i * virt) & (lane < (i + 1) * virt), occ_ref[i], levels)
    empty = jnp.zeros((8, cols), jnp.float32)
    for i in range(virt):
        empty = jnp.where((lane & (virt - 1)) == i, virt_ref[i], empty)
    kept = jnp.where(row == 1, kept_ref[0].astype(jnp.float32), kept_ref[1].astype(jnp.float32))
    infos[0] = jnp.where(row == 0, levels - empty, kept)
    info_copies = [
        remote(infos.at[0], infos.at[i], info_s.at[i - 1], info_r.at[i - 1], (device, a))
        for i, device in ((1, partner), (2, xt), (3, xd))
    ]
    for copy in info_copies:
        copy.start()

    def clear(i, _):
        s[i] = jnp.zeros(s.shape[1:], jnp.float32)
        return 0

    lax.fori_loop(0, 4, clear, 0)
    for copy in own:
        copy.wait()

    def add_pair(index, value):
        s[index] += value.reshape(2, 4, piece, cols)

    def held(block, k):
        return zhi[block, place(k)], zlo[block, place(k)]

    def divide(block, k):
        value = z[block, place(k)] if block < OWN else out_ref[source(side_t if block == OWN else side_d, k)]
        zhi[block, place(k)], zlo[block, place(k)] = split(value)

    def fetch(k, _):
        divide(OWN, k)
        divide(OWN_D, k)
        for i, block in enumerate(arrivals):
            landed(z.at[block, place(k)], f_r.at[i, k])

        @pl.when(k + WINDOW < count)
        def _():
            for copy in send_copies(k):
                copy.wait_send()
            for copy in send_copies(k + WINDOW):
                copy.start()

        for block in arrivals:
            divide(block, k)
        found = dot3(held(T - yl, k), beside(held(OWN, k), held(Y + yl, k)), ROWS)
        add_pair(1 + yl, found[:, :cols])
        add_pair(3, found[:, cols:])
        add_pair(2 - yl, dot3(held(ol * OWN + yl * T, k), held(ol * Y + yl * OWN, k), ROWS))
        add_pair(0, dot3(held(OWN_D, k), held(D, k), ROWS))
        return 0

    lax.fori_loop(0, count, fetch, 0)

    order = (3, 2, 1, 0)
    step_a = {b: remote(s.at[b, 1 - c], ra.at[b], a_s.at[b], a_r.at[b], core) for b in order}
    for b in order:
        step_a[b].start()
    mine = [2 * site[b] + yh for b in range(4)]

    def members(b):
        far = ((o, there), 2 * site[b] + 1 - yh, b)
        same = ((others[b], here), 2 * (1 - site[b]) + yh, tile_there[b])
        other = ((others[b], there), 2 * (1 - site[b]) + 1 - yh, tile_there[b])
        return ((same, far, other), (same, far, other), (same, other, far), (other, same, far))[b]

    step_b, step_next = {}, {}
    for b in order:
        (p1, q1, t1), (p2, q2, t2), (_, q3, _) = members(b)
        step_b[b] = [
            remote(s.at[b, c, q3], rb.at[t1, 1], b_s.at[b, 1], b_r.at[t1, 1], p1),
            remote(s.at[b, c, q1], rb.at[t1, 0], b_s.at[b, 0], b_r.at[t1, 0], p1),
        ]
        step_next[b] = remote(s.at[b, c, q2], rb.at[t2, 2], b_s.at[b, 2], b_r.at[t2, 2], p2)
    for b in order:
        step_a[b].wait()
        s[b, c] += ra[b]
        for copy in step_b[b]:
            copy.start()
    for b in order:
        q2 = members(b)[1][1]
        landed(rb.at[b, 1], b_r.at[b, 1])
        s[b, c, q2] += rb[b, 1]
        step_next[b].start()

    for i in range(3):
        landed(infos.at[i + 1], info_r.at[i])
    row = lax.broadcasted_iota(jnp.int32, (piece, cols), 0)
    lane = lax.broadcasted_iota(jnp.int32, (piece, cols), 1)
    row_info, col_info = (0, 2, yl, 2 - yl), (3, 0, ol, 1 + yl)
    kept_info, distance = (3 * yl, 2 * ol, ol, 2 - yl), (2, 2, 1, 1)

    def hand_on(b, q, i, to):
        device, _, t = members(b)[to]
        return remote(ag.at[b, c, q], ag.at[t, c, q], g_s.at[b, i], g_r.at[t, i], device)

    step_g = {
        b: [hand_on(b, mine[b], 0, 1), hand_on(b, mine[b], 1, 0), hand_on(b, members(b)[1][1], 2, 0)] for b in order
    }

    def core_copy(b, q):
        return remote(ag.at[b, c, q], ag.at[b, c, q], c_s.at[b, q], c_r.at[b, q], core)

    for b in order:
        first = (c * 4 + mine[b]) * piece
        level = jnp.sum(jnp.where(lane == row + first, infos[row_info[b], pl.ds(0, 1)], 0.0), axis=1, keepdims=True)
        gap = level + infos[col_info[b], pl.ds(0, 1)]
        for i in (0, 2):
            landed(rb.at[b, i], b_r.at[b, i])
        block = s[b, c, mine[b]] + rb[b, 0] + rb[b, 2]
        swapped = jnp.concatenate([swap_virtuals(block[:, i : i + 128], virt) for i in range(0, cols, 128)], axis=1)
        ag[b, c, mine[b]] = infos[kept_info[b], pl.ds(distance[b], 1)] * (2.0 * block - swapped) / gap
        for copy in step_g[b][:2]:
            copy.start()
        core_copy(b, mine[b]).start()

    for b in order:
        q2 = members(b)[1][1]
        landed(ag.at[b, c, q2], g_r.at[b, 0])
        step_g[b][2].start()
        core_copy(b, q2).start()

    def sent(k, _):
        for copy in send_copies(k):
            copy.wait_send()
        return 0

    lax.fori_loop(count - WINDOW, count, sent, 0)
    for copy in info_copies:
        copy.wait_send()
    for b in order:
        (_, q1, _), _, (_, q3, _) = members(b)
        for q, i in ((q1, 1), (q3, 2)):
            landed(ag.at[b, c, q], g_r.at[b, i])
            core_copy(b, q).start()

    def whole(b):
        for q in range(4):
            landed(ag.at[b, 1 - c, q], c_r.at[b, q])
        return ag[b].reshape(cols, cols)

    left, right = pl.ds(0, cols), pl.ds(cols, cols)
    t_to_y, own_to_y = whole(3), whole(2)

    @pl.when(yl == 0)
    def _():
        mah[:, right], mal[:, right] = split(t_to_y)
        mbh[right, :], mbl[right, :] = split(t_to_y)
        mbh[left, :], mbl[left, :] = split(own_to_y)

    @pl.when(yl == 1)
    def _():
        turned = t_to_y.T
        mah[:, right], mal[:, right] = split(turned)
        mbh[right, :], mbl[right, :] = split(turned)
        mbh[left, :], mbl[left, :] = split(own_to_y.T)

    mah[:, left], mal[:, left] = split(whole(1))
    mdh[...], mdl[...] = split(whole(0))

    def give_copies(k):
        return (
            remote(rbuf.at[0, place(k)], z.at[Y, place(k)], r_s.at[0, k], r_r.at[0, k], (partner, a)),
            remote(rbuf.at[1, place(k)], z.at[T, place(k)], r_s.at[1, k], r_r.at[1, k], (xd, a)),
            remote(rbuf.at[2, place(k)], z.at[D, place(k)], r_s.at[2, k], r_r.at[2, k], (xt, a)),
        )

    def finish(k, _):
        @pl.when(k < count)
        def _():
            @pl.when(k >= WINDOW)
            def _():
                for copy in give_copies(k - WINDOW):
                    copy.wait_send()

            y, t, d, own_t, own_d = (held(block, k) for block in range(5))
            rbuf[0, place(k)] = dot3(beside(own_t, t), (mbh[...], mbl[...]), PLAIN)
            rbuf[1, place(k)] = dot3(beside(own_t, y), (mah[...], mal[...]), TURNED)
            rbuf[2, place(k)] = dot3(own_d, (mdh[...], mdl[...]), PLAIN)
            for copy in give_copies(k):
                copy.start()
            out_ref[source(side_t, k)] = dot3(t, (mah[:, left], mal[:, left]), PLAIN) + dot3(
                y, (mbh[left, :], mbl[left, :]), TURNED
            )
            out_ref[source(side_d, k)] = dot3(d, (mdh[...], mdl[...]), TURNED)

        @pl.when(k >= LAG)
        def _():
            j = k - LAG
            for i, block in enumerate(arrivals):
                landed(z.at[block, place(j)], r_r.at[i, j])
            out_ref[source(side_t, j)] += z[T, place(j)]
            out_ref[source(side_d, j)] += z[Y, place(j)] + z[D, place(j)]

        return 0

    lax.fori_loop(0, count + LAG, finish, 0)

    def given(k, _):
        for copy in give_copies(k):
            copy.wait_send()
        return 0

    lax.fori_loop(count - WINDOW, count, given, 0)
    for b in order:
        for copy in step_b[b] + [step_next[b]] + step_g[b]:
            copy.wait_send()
        for q in range(4):
            core_copy(b, q).wait_send()


def solution(mesh):
    n_occ = mesh.shape["occ"]

    def shards(three_centre, occ_energy, virt_energy, pair_kept):
        rows, cols = three_centre.shape
        half, chunk = rows // 2, rows // 16
        count = half // chunk
        piece = (cols // 8, cols)
        f32, bf16 = jnp.float32, jnp.bfloat16
        dma = pltpu.SemaphoreType.DMA
        return pl.pallas_call(
            functools.partial(kernel, n_occ, chunk),
            out_shape=pltpu.VMEM((rows, cols), f32),
            in_specs=[pl.BlockSpec(memory_space=pltpu.SMEM)] * 3 + [pl.BlockSpec(memory_space=pl.ANY)],
            out_specs=pl.BlockSpec(memory_space=pltpu.VMEM),
            scratch_shapes=[
                pltpu.VMEM((3, half, cols), f32),
                pltpu.VMEM((5, half, cols), bf16),
                pltpu.VMEM((5, half, cols), bf16),
                pltpu.VMEM((4, 2, 4) + piece, f32),
                pltpu.VMEM((4, 4) + piece, f32),
                pltpu.VMEM((4, 3) + piece, f32),
                pltpu.VMEM((4, 2, 4) + piece, f32),
                pltpu.VMEM((cols, cols), bf16),
                pltpu.VMEM((cols, cols), bf16),
                pltpu.VMEM((cols, 2 * cols), bf16),
                pltpu.VMEM((cols, 2 * cols), bf16),
                pltpu.VMEM((2 * cols, cols), bf16),
                pltpu.VMEM((2 * cols, cols), bf16),
                pltpu.VMEM((3, half, cols), f32),
                pltpu.VMEM((4, 8, cols), f32),
                dma((3,)), dma((3,)),
                dma((3, count)), dma((3, count)), dma((2,)),
                dma((4,)), dma((4,)),
                dma((4, 3)), dma((4, 3)),
                dma((4, 3)), dma((4, 3)),
                dma((4, 4)), dma((4, 4)),
                dma((3, count)), dma((3, count)),
            ],
            compiler_params=pltpu.CompilerParams(
                collective_id=0, has_side_effects=True, vmem_limit_bytes=54 * 2**20
            ),
        )(occ_energy, virt_energy, pair_kept.reshape(-1), three_centre)

    return jax.shard_map(
        shards,
        mesh=mesh,
        in_specs=(P("aux", "occ"), P("occ"), P(), P(None, "occ")),
        out_specs=P("aux", "occ"),
        check_vma=False,
    )
```

```python
import functools

import jax
import jax.numpy as jnp
from jax import lax
from jax.experimental import pallas as pl
from jax.experimental.pallas import tpu as pltpu
from jax.sharding import PartitionSpec as P

MESH = pl.DeviceIdType.MESH
Y, T, D, OWN, OWN_D = range(5)
WINDOW = 3
LAG = 3


def split(x):
    high = x.astype(jnp.bfloat16)
    return high, (x - high.astype(jnp.float32)).astype(jnp.bfloat16)


def dot3(a, b, dims):
    def one(x, y):
        return lax.dot_general(x, y, (dims, ((), ())), preferred_element_type=jnp.float32)

    return one(a[0], b[0]) + one(a[0], b[1]) + one(a[1], b[0])


ROWS = ((0,), (0,))
PLAIN = ((1,), (0,))
TURNED = ((1,), (1,))


def beside(a, b):
    return tuple(jnp.concatenate([x, y], axis=1) for x, y in zip(a, b))


def swap_virtuals(x, virt):
    rows, lanes = x.shape
    row = lax.broadcasted_iota(jnp.int32, x.shape, 0)
    lane = lax.broadcasted_iota(jnp.int32, x.shape, 1)
    step = 1
    while step < virt:
        row_bit, lane_bit = (row & step) != 0, (lane & step) != 0
        from_above = pltpu.roll(pltpu.roll(x, step, 0), lanes - step, 1)
        from_below = pltpu.roll(pltpu.roll(x, rows - step, 0), step, 1)
        moved = jnp.where(row_bit, from_above, from_below)
        x = jnp.where(row_bit == lane_bit, x, moved)
        step *= 2
    return x


def kernel(
    n_occ, chunk,
    occ_ref, virt_ref, kept_ref, b_ref, out_ref,
    z, zhi, zlo, s, ra, rb, ag, mdh, mdl, mah, mal, mbh, mbl, rbuf, infos, factor,
    info_s, info_r, f_s, f_r, l_s, a_s, a_r, b_s, b_r, g_s, g_r, c_s, c_r, r_s, r_r,
):
    rows, cols = b_ref.shape
    half = rows // 2
    count = half // chunk
    piece = cols // 8
    occ, virt = occ_ref.shape[0], virt_ref.shape[0]

    o, a = lax.axis_index("occ"), lax.axis_index("aux")
    yl, c, yh = lax.rem(o, 2), lax.rem(a, 2), lax.div(a, 2)
    ol, m2 = 1 - yl, o - lax.rem(o, 2)
    up, down = lax.rem(m2 + 2, n_occ), lax.rem(m2 + n_occ - 2, n_occ)
    toward, away = ol * up + yl * down, ol * down + yl * up
    core = (o, a + 1 - 2 * c)
    here, there = a, 2 * (1 - yh) + c
    xd, xt, partner, diagonal = toward + yl, away + yl, m2 + ol, toward + ol
    others = (xt, xd, partner, diagonal)
    tile_there = (1, 0, 2, 3)
    site = (0, 1, yl, yl)

    barrier = pltpu.get_barrier_semaphore()
    everyone = [core, (o, there)] + [(x, y) for x in others for y in (here, there)]
    for device in everyone:
        pl.semaphore_signal(barrier, inc=1, device_id=device, device_id_type=MESH)

    def remote(src, dst, ss, rs, device):
        return pltpu.make_async_remote_copy(
            src_ref=src, dst_ref=dst, send_sem=ss, recv_sem=rs, device_id=device, device_id_type=MESH
        )

    def landed(dst, rs):
        remote(dst, dst, rs, rs, (partner, a)).wait_recv()

    def place(k):
        return pl.ds(pl.multiple_of(k * chunk, chunk), chunk)

    def source(side, k):
        return pl.ds(pl.multiple_of(side * half + k * chunk, chunk), chunk)

    side_t, side_d = ol, yl

    def send_copies(k):
        return (
            remote(b_ref.at[source(side_d, k)], z.at[Y, place(k)], f_s.at[0, k], f_r.at[0, k], (partner, a)),
            remote(b_ref.at[source(side_t, k)], z.at[T, place(k)], f_s.at[1, k], f_r.at[1, k], (xt, a)),
            remote(b_ref.at[source(side_d, k)], z.at[D, place(k)], f_s.at[2, k], f_r.at[2, k], (xd, a)),
        )

    arrivals = (Y, T, D)
    own = [
        pltpu.make_async_copy(b_ref.at[pl.ds(side_t * half, half)], out_ref.at[pl.ds(side_t * half, half)], l_s.at[0]),
        pltpu.make_async_copy(b_ref.at[pl.ds(side_d * half, half)], out_ref.at[pl.ds(side_d * half, half)], l_s.at[1]),
    ]
    for copy in own:
        copy.start()

    row = lax.broadcasted_iota(jnp.int32, (8, cols), 0)
    lane = lax.broadcasted_iota(jnp.int32, (8, cols), 1)
    levels = jnp.zeros((8, cols), jnp.float32)
    for i in range(occ):
        levels = jnp.where((lane >= i * virt) & (lane < (i + 1) * virt), occ_ref[i], levels)
    empty = jnp.zeros((8, cols), jnp.float32)
    for i in range(virt):
        empty = jnp.where((lane & (virt - 1)) == i, virt_ref[i], empty)
    kept = jnp.where(row == 1, kept_ref[0].astype(jnp.float32), kept_ref[1].astype(jnp.float32))
    infos[0] = jnp.where(row == 0, levels - empty, kept)
    info_copies = [
        remote(infos.at[0], infos.at[i], info_s.at[i - 1], info_r.at[i - 1], (device, a))
        for i, device in ((1, partner), (2, xt), (3, xd))
    ]

    pl.semaphore_wait(barrier, len(everyone))
    for k in range(WINDOW):
        for copy in send_copies(k):
            copy.start()
    for copy in info_copies:
        copy.start()

    def clear(i, _):
        s[i] = jnp.zeros(s.shape[1:], jnp.float32)
        return 0

    lax.fori_loop(0, 4, clear, 0)

    for i in range(3):
        landed(infos.at[i + 1], info_r.at[i])
    mine = [2 * site[b] + yh for b in range(4)]
    row_info, col_info = (0, 2, yl, 2 - yl), (3, 0, ol, 1 + yl)
    kept_info, distance = (3 * yl, 2 * ol, ol, 2 - yl), (2, 2, 1, 1)
    row = lax.broadcasted_iota(jnp.int32, (piece, cols), 0)
    lane = lax.broadcasted_iota(jnp.int32, (piece, cols), 1)
    for b in range(4):
        first = (c * 4 + mine[b]) * piece
        level = jnp.sum(jnp.where(lane == row + first, infos[row_info[b], pl.ds(0, 1)], 0.0), axis=1, keepdims=True)
        gap = level + infos[col_info[b], pl.ds(0, 1)]
        factor[b] = infos[kept_info[b], pl.ds(distance[b], 1)] / gap
    for copy in own:
        copy.wait()

    def add_pair(index, value):
        s[index] += value.reshape(2, 4, piece, cols)

    def held(block, k):
        return zhi[block, place(k)], zlo[block, place(k)]

    def divide(block, k):
        value = z[block, place(k)] if block < OWN else out_ref[source(side_t if block == OWN else side_d, k)]
        zhi[block, place(k)], zlo[block, place(k)] = split(value)

    def arrive(k):
        divide(OWN, k)
        divide(OWN_D, k)
        for i, block in enumerate(arrivals):
            landed(z.at[block, place(k)], f_r.at[i, k])

        @pl.when(k + WINDOW < count)
        def _():
            for copy in send_copies(k):
                copy.wait_send()
            for copy in send_copies(k + WINDOW):
                copy.start()

        for block in arrivals:
            divide(block, k)

    def pairs_t(k):
        found = dot3(held(T - yl, k), beside(held(OWN, k), held(Y + yl, k)), ROWS)
        add_pair(1 + yl, found[:, :cols])
        add_pair(3, found[:, cols:])

    def pairs_own(k):
        add_pair(2 - yl, dot3(held(ol * OWN + yl * T, k), held(ol * Y + yl * OWN, k), ROWS))

    def pairs_d(k):
        add_pair(0, dot3(held(OWN_D, k), held(D, k), ROWS))

    def fetch(k, _):
        arrive(k)
        pairs_t(k)
        pairs_own(k)
        pairs_d(k)
        return 0

    lax.fori_loop(0, count - 1, fetch, 0)

    order = (3, 2, 1, 0)

    def to_core(b):
        return remote(s.at[b, 1 - c], ra.at[b], a_s.at[b], a_r.at[b], core)

    def members(b):
        far = ((o, there), 2 * site[b] + 1 - yh, b)
        same = ((others[b], here), 2 * (1 - site[b]) + yh, tile_there[b])
        other = ((others[b], there), 2 * (1 - site[b]) + 1 - yh, tile_there[b])
        return ((same, far, other), (same, far, other), (same, other, far), (other, same, far))[b]

    step_b, step_next = {}, {}
    for b in order:
        (p1, q1, t1), (p2, q2, t2), (_, q3, _) = members(b)
        step_b[b] = [
            remote(s.at[b, c, q3], rb.at[t1, 1], b_s.at[b, 1], b_r.at[t1, 1], p1),
            remote(s.at[b, c, q1], rb.at[t1, 0], b_s.at[b, 0], b_r.at[t1, 0], p1),
        ]
        step_next[b] = remote(s.at[b, c, q2], rb.at[t2, 2], b_s.at[b, 2], b_r.at[t2, 2], p2)

    def halve(b):
        to_core(b).wait()
        s[b, c] += ra[b]
        for copy in step_b[b]:
            copy.start()

    arrive(count - 1)
    pairs_t(count - 1)
    to_core(3).start()
    to_core(1 + yl).start()
    pairs_own(count - 1)
    to_core(2 - yl).start()
    halve(3)
    pairs_d(count - 1)
    to_core(0).start()
    for b in (2, 1, 0):
        halve(b)
    for b in order:
        q2 = members(b)[1][1]
        landed(rb.at[b, 1], b_r.at[b, 1])
        s[b, c, q2] += rb[b, 1]
        step_next[b].start()

    def hand_on(b, q, i, to):
        device, _, t = members(b)[to]
        return remote(ag.at[b, c, q], ag.at[t, c, q], g_s.at[b, i], g_r.at[t, i], device)

    step_g = {
        b: [hand_on(b, mine[b], 0, 1), hand_on(b, mine[b], 1, 0), hand_on(b, members(b)[1][1], 2, 0)] for b in order
    }

    def core_copy(b, q):
        return remote(ag.at[b, c, q], ag.at[b, c, q], c_s.at[b, q], c_r.at[b, q], core)

    for b in order:
        for i in (0, 2):
            landed(rb.at[b, i], b_r.at[b, i])
        block = s[b, c, mine[b]] + rb[b, 0] + rb[b, 2]
        swapped = jnp.concatenate([swap_virtuals(block[:, i : i + 128], virt) for i in range(0, cols, 128)], axis=1)
        ag[b, c, mine[b]] = factor[b] * (2.0 * block - swapped)
        for copy in step_g[b][:2]:
            copy.start()
        core_copy(b, mine[b]).start()

    for b in order:
        q2 = members(b)[1][1]
        landed(ag.at[b, c, q2], g_r.at[b, 0])
        step_g[b][2].start()
        core_copy(b, q2).start()

    def sent(k, _):
        for copy in send_copies(k):
            copy.wait_send()
        return 0

    lax.fori_loop(count - WINDOW, count, sent, 0)
    for copy in info_copies:
        copy.wait_send()

    def forward(b):
        (_, q1, _), _, (_, q3, _) = members(b)
        for q, i in ((q1, 1), (q3, 2)):
            landed(ag.at[b, c, q], g_r.at[b, i])
            core_copy(b, q).start()

    def whole(b):
        for q in range(4):
            landed(ag.at[b, 1 - c, q], c_r.at[b, q])
        return ag[b].reshape(cols, cols)

    left, right = pl.ds(0, cols), pl.ds(cols, cols)

    def give_copies(k):
        return (
            remote(rbuf.at[0, place(k)], z.at[Y, place(k)], r_s.at[0, k], r_r.at[0, k], (partner, a)),
            remote(rbuf.at[1, place(k)], z.at[T, place(k)], r_s.at[1, k], r_r.at[1, k], (xd, a)),
            remote(rbuf.at[2, place(k)], z.at[D, place(k)], r_s.at[2, k], r_r.at[2, k], (xt, a)),
        )

    def give_y(k):
        rbuf[0, place(k)] = dot3(beside(held(OWN, k), held(T, k)), (mbh[...], mbl[...]), PLAIN)
        give_copies(k)[0].start()

    def give_t(k):
        rbuf[1, place(k)] = dot3(beside(held(OWN, k), held(Y, k)), (mah[...], mal[...]), TURNED)
        give_copies(k)[1].start()

    def give_d(k):
        rbuf[2, place(k)] = dot3(held(OWN_D, k), (mdh[...], mdl[...]), PLAIN)
        give_copies(k)[2].start()

    for b in (3, 2, 1):
        forward(b)
    t_to_y, own_to_y = whole(3), whole(2)

    @pl.when(yl == 0)
    def _():
        mah[:, right], mal[:, right] = split(t_to_y)
        mbh[right, :], mbl[right, :] = split(t_to_y)
        mbh[left, :], mbl[left, :] = split(own_to_y)

    @pl.when(yl == 1)
    def _():
        turned = t_to_y.T
        mah[:, right], mal[:, right] = split(turned)
        mbh[right, :], mbl[right, :] = split(turned)
        mbh[left, :], mbl[left, :] = split(own_to_y.T)

    give_y(0)
    mah[:, left], mal[:, left] = split(whole(1))
    give_t(0)
    forward(0)
    mdh[...], mdl[...] = split(whole(0))
    give_d(0)

    def finish(k, _):
        @pl.when((k > 0) & (k < count))
        def _():
            @pl.when(k >= WINDOW)
            def _():
                for copy in give_copies(k - WINDOW):
                    copy.wait_send()

            give_y(k)
            give_t(k)
            give_d(k)

        @pl.when(k < count)
        def _():
            y, t, d = (held(block, k) for block in arrivals)
            out_ref[source(side_t, k)] = dot3(t, (mah[:, left], mal[:, left]), PLAIN) + dot3(
                y, (mbh[left, :], mbl[left, :]), TURNED
            )
            out_ref[source(side_d, k)] = dot3(d, (mdh[...], mdl[...]), TURNED)

        @pl.when(k >= LAG)
        def _():
            j = k - LAG
            for i, block in enumerate(arrivals):
                landed(z.at[block, place(j)], r_r.at[i, j])
            out_ref[source(side_t, j)] += z[T, place(j)]
            out_ref[source(side_d, j)] += z[Y, place(j)] + z[D, place(j)]

        return 0

    lax.fori_loop(0, count + LAG, finish, 0)

    def given(k, _):
        for copy in give_copies(k):
            copy.wait_send()
        return 0

    lax.fori_loop(count - WINDOW, count, given, 0)
    for b in order:
        for copy in step_b[b] + [step_next[b]] + step_g[b]:
            copy.wait_send()
        for q in range(4):
            core_copy(b, q).wait_send()


def solution(mesh):
    n_occ = mesh.shape["occ"]

    def shards(three_centre, occ_energy, virt_energy, pair_kept):
        rows, cols = three_centre.shape
        half, chunk = rows // 2, rows // 16
        count = half // chunk
        piece = (cols // 8, cols)
        f32, bf16 = jnp.float32, jnp.bfloat16
        dma = pltpu.SemaphoreType.DMA
        return pl.pallas_call(
            functools.partial(kernel, n_occ, chunk),
            out_shape=pltpu.VMEM((rows, cols), f32),
            in_specs=[pl.BlockSpec(memory_space=pltpu.SMEM)] * 3 + [pl.BlockSpec(memory_space=pl.ANY)],
            out_specs=pl.BlockSpec(memory_space=pltpu.VMEM),
            scratch_shapes=[
                pltpu.VMEM((3, half, cols), f32),
                pltpu.VMEM((5, half, cols), bf16),
                pltpu.VMEM((5, half, cols), bf16),
                pltpu.VMEM((4, 2, 4) + piece, f32),
                pltpu.VMEM((4, 4) + piece, f32),
                pltpu.VMEM((4, 3) + piece, f32),
                pltpu.VMEM((4, 2, 4) + piece, f32),
                pltpu.VMEM((cols, cols), bf16),
                pltpu.VMEM((cols, cols), bf16),
                pltpu.VMEM((cols, 2 * cols), bf16),
                pltpu.VMEM((cols, 2 * cols), bf16),
                pltpu.VMEM((2 * cols, cols), bf16),
                pltpu.VMEM((2 * cols, cols), bf16),
                pltpu.VMEM((3, half, cols), f32),
                pltpu.VMEM((4, 8, cols), f32),
                pltpu.VMEM((4,) + piece, f32),
                dma((3,)), dma((3,)),
                dma((3, count)), dma((3, count)), dma((2,)),
                dma((4,)), dma((4,)),
                dma((4, 3)), dma((4, 3)),
                dma((4, 3)), dma((4, 3)),
                dma((4, 4)), dma((4, 4)),
                dma((3, count)), dma((3, count)),
            ],
            compiler_params=pltpu.CompilerParams(
                collective_id=0, has_side_effects=True, vmem_limit_bytes=54 * 2**20
            ),
        )(occ_energy, virt_energy, pair_kept.reshape(-1), three_centre)

    return jax.shard_map(
        shards,
        mesh=mesh,
        in_specs=(P("aux", "occ"), P("occ"), P(), P(None, "occ")),
        out_specs=P("aux", "occ"),
        check_vma=False,
    )
```

```python
import functools

import jax
import jax.numpy as jnp
from jax import lax
from jax.experimental import pallas as pl
from jax.experimental.pallas import tpu as pltpu
from jax.sharding import PartitionSpec as P

MESH = pl.DeviceIdType.MESH
Y, T, D, OWN, OWN_D = range(5)
PARTS = 2
WINDOW = 2
LAG = 2


def split(x):
    high = x.astype(jnp.bfloat16)
    return high, (x - high.astype(jnp.float32)).astype(jnp.bfloat16)


def dot3(a, b, dims):
    def one(x, y):
        return lax.dot_general(x, y, (dims, ((), ())), preferred_element_type=jnp.float32)

    return one(a[0], b[0]) + one(a[0], b[1]) + one(a[1], b[0])


ROWS = ((0,), (0,))
PLAIN = ((1,), (0,))
TURNED = ((1,), (1,))


def beside(a, b):
    return tuple(jnp.concatenate([x, y], axis=1) for x, y in zip(a, b))


def swap_virtuals(x, virt):
    rows, lanes = x.shape
    row = lax.broadcasted_iota(jnp.int32, x.shape, 0)
    lane = lax.broadcasted_iota(jnp.int32, x.shape, 1)
    step = 1
    while step < virt:
        row_bit, lane_bit = (row & step) != 0, (lane & step) != 0
        from_above = pltpu.roll(pltpu.roll(x, step, 0), lanes - step, 1)
        from_below = pltpu.roll(pltpu.roll(x, rows - step, 0), step, 1)
        moved = jnp.where(row_bit, from_above, from_below)
        x = jnp.where(row_bit == lane_bit, x, moved)
        step *= 2
    return x


def kernel(
    n_occ, chunk,
    occ_ref, virt_ref, kept_ref, b_ref, out_ref,
    z, zhi, zlo, s, ra, rb, ag, mdh, mdl, mah, mal, mbh, mbl, rbuf, infos, factor,
    info_s, info_r, f_s, f_r, l_s, a_s, a_r, b_s, b_r, g_s, g_r, c_s, c_r, r_s, r_r,
):
    rows, cols = b_ref.shape
    half = rows // 2
    count = half // chunk
    piece = cols // 8
    occ, virt = occ_ref.shape[0], virt_ref.shape[0]

    o, a = lax.axis_index("occ"), lax.axis_index("aux")
    yl, c, yh = lax.rem(o, 2), lax.rem(a, 2), lax.div(a, 2)
    ol, m2 = 1 - yl, o - lax.rem(o, 2)
    up, down = lax.rem(m2 + 2, n_occ), lax.rem(m2 + n_occ - 2, n_occ)
    toward, away = ol * up + yl * down, ol * down + yl * up
    core = (o, a + 1 - 2 * c)
    here, there = a, 2 * (1 - yh) + c
    xd, xt, partner, diagonal = toward + yl, away + yl, m2 + ol, toward + ol
    others = (xt, xd, partner, diagonal)
    tile_there = (1, 0, 2, 3)
    site = (0, 1, yl, yl)

    barrier = pltpu.get_barrier_semaphore()
    everyone = [core, (o, there)] + [(x, y) for x in others for y in (here, there)]
    for device in everyone:
        pl.semaphore_signal(barrier, inc=1, device_id=device, device_id_type=MESH)

    def remote(src, dst, ss, rs, device):
        return pltpu.make_async_remote_copy(
            src_ref=src, dst_ref=dst, send_sem=ss, recv_sem=rs, device_id=device, device_id_type=MESH
        )

    def landed(dst, rs):
        remote(dst, dst, rs, rs, (partner, a)).wait_recv()

    def place(k):
        return pl.ds(pl.multiple_of(k * chunk, chunk), chunk)

    def source(side, k):
        return pl.ds(pl.multiple_of(side * half + k * chunk, chunk), chunk)

    side_t, side_d = ol, yl

    part = chunk // PARTS

    def part_place(k):
        return pl.ds(pl.multiple_of(k * part, part), part)

    def send_copies(k):
        own_t = b_ref.at[pl.ds(pl.multiple_of(side_t * half + k * part, part), part)]
        own_d = b_ref.at[pl.ds(pl.multiple_of(side_d * half + k * part, part), part)]
        return (
            remote(own_d, z.at[Y, part_place(k)], f_s.at[0, k], f_r.at[0, k], (partner, a)),
            remote(own_t, z.at[T, part_place(k)], f_s.at[1, k], f_r.at[1, k], (xt, a)),
            remote(own_d, z.at[D, part_place(k)], f_s.at[2, k], f_r.at[2, k], (xd, a)),
        )

    arrivals = (Y, T, D)
    own = [
        pltpu.make_async_copy(b_ref.at[pl.ds(side_t * half, half)], out_ref.at[pl.ds(side_t * half, half)], l_s.at[0]),
        pltpu.make_async_copy(b_ref.at[pl.ds(side_d * half, half)], out_ref.at[pl.ds(side_d * half, half)], l_s.at[1]),
    ]
    for copy in own:
        copy.start()

    row = lax.broadcasted_iota(jnp.int32, (8, cols), 0)
    lane = lax.broadcasted_iota(jnp.int32, (8, cols), 1)
    levels = jnp.zeros((8, cols), jnp.float32)
    for i in range(occ):
        levels = jnp.where((lane >= i * virt) & (lane < (i + 1) * virt), occ_ref[i], levels)
    empty = jnp.zeros((8, cols), jnp.float32)
    for i in range(virt):
        empty = jnp.where((lane & (virt - 1)) == i, virt_ref[i], empty)
    kept = jnp.where(row == 1, kept_ref[0].astype(jnp.float32), kept_ref[1].astype(jnp.float32))
    infos[0] = jnp.where(row == 0, levels - empty, kept)
    info_copies = [
        remote(infos.at[0], infos.at[i], info_s.at[i - 1], info_r.at[i - 1], (device, a))
        for i, device in ((1, partner), (2, xt), (3, xd))
    ]

    pl.semaphore_wait(barrier, len(everyone))
    for k in range(WINDOW):
        for copy in send_copies(k):
            copy.start()
    for copy in info_copies:
        copy.start()

    def clear(i, _):
        s[i] = jnp.zeros(s.shape[1:], jnp.float32)
        return 0

    lax.fori_loop(0, 4, clear, 0)

    for i in range(3):
        landed(infos.at[i + 1], info_r.at[i])
    mine = [2 * site[b] + yh for b in range(4)]
    row_info, col_info = (0, 2, yl, 2 - yl), (3, 0, ol, 1 + yl)
    kept_info, distance = (3 * yl, 2 * ol, ol, 2 - yl), (2, 2, 1, 1)
    row = lax.broadcasted_iota(jnp.int32, (piece, cols), 0)
    lane = lax.broadcasted_iota(jnp.int32, (piece, cols), 1)
    for b in range(4):
        first = (c * 4 + mine[b]) * piece
        level = jnp.sum(jnp.where(lane == row + first, infos[row_info[b], pl.ds(0, 1)], 0.0), axis=1, keepdims=True)
        gap = level + infos[col_info[b], pl.ds(0, 1)]
        factor[b] = infos[kept_info[b], pl.ds(distance[b], 1)] / gap
    for copy in own:
        copy.wait()

    def add_pair(index, value):
        s[index] += value.reshape(2, 4, piece, cols)

    def held(block, k):
        return zhi[block, place(k)], zlo[block, place(k)]

    def divide(block, k):
        zhi[block, place(k)], zlo[block, place(k)] = split(out_ref[source(side_t if block == OWN else side_d, k)])

    def arrive(k):
        divide(OWN, k)
        divide(OWN_D, k)
        for step in range(PARTS):
            j = k * PARTS + step
            for i, block in enumerate(arrivals):
                landed(z.at[block, part_place(j)], f_r.at[i, j])

            @pl.when(j + WINDOW < count * PARTS)
            def _():
                for copy in send_copies(j):
                    copy.wait_send()
                for copy in send_copies(j + WINDOW):
                    copy.start()

            for block in arrivals:
                zhi[block, part_place(j)], zlo[block, part_place(j)] = split(z[block, part_place(j)])

    def pairs_t(k):
        found = dot3(held(T - yl, k), beside(held(OWN, k), held(Y + yl, k)), ROWS)
        add_pair(1 + yl, found[:, :cols])
        add_pair(3, found[:, cols:])

    def pairs_own(k):
        add_pair(2 - yl, dot3(held(ol * OWN + yl * T, k), held(ol * Y + yl * OWN, k), ROWS))

    def pairs_d(k):
        add_pair(0, dot3(held(OWN_D, k), held(D, k), ROWS))

    def fetch(k, _):
        arrive(k)
        pairs_t(k)
        pairs_own(k)
        pairs_d(k)
        return 0

    lax.fori_loop(0, count - 1, fetch, 0)

    order = (3, 2, 1, 0)

    def to_core(b):
        return remote(s.at[b, 1 - c], ra.at[b], a_s.at[b], a_r.at[b], core)

    def members(b):
        far = ((o, there), 2 * site[b] + 1 - yh, b)
        same = ((others[b], here), 2 * (1 - site[b]) + yh, tile_there[b])
        other = ((others[b], there), 2 * (1 - site[b]) + 1 - yh, tile_there[b])
        return ((same, far, other), (same, far, other), (same, other, far), (other, same, far))[b]

    step_b, step_next = {}, {}
    for b in order:
        (p1, q1, t1), (p2, q2, t2), (_, q3, _) = members(b)
        step_b[b] = [
            remote(s.at[b, c, q3], rb.at[t1, 1], b_s.at[b, 1], b_r.at[t1, 1], p1),
            remote(s.at[b, c, q1], rb.at[t1, 0], b_s.at[b, 0], b_r.at[t1, 0], p1),
        ]
        step_next[b] = remote(s.at[b, c, q2], rb.at[t2, 2], b_s.at[b, 2], b_r.at[t2, 2], p2)

    def halve(b):
        to_core(b).wait()
        s[b, c] += ra[b]
        for copy in step_b[b]:
            copy.start()

    arrive(count - 1)
    pairs_t(count - 1)
    to_core(3).start()
    to_core(1 + yl).start()
    pairs_own(count - 1)
    to_core(2 - yl).start()
    halve(3)
    pairs_d(count - 1)
    to_core(0).start()
    for b in (2, 1, 0):
        halve(b)
    for b in order:
        q2 = members(b)[1][1]
        landed(rb.at[b, 1], b_r.at[b, 1])
        s[b, c, q2] += rb[b, 1]
        step_next[b].start()

    def hand_on(b, q, i, to):
        device, _, t = members(b)[to]
        return remote(ag.at[b, c, q], ag.at[t, c, q], g_s.at[b, i], g_r.at[t, i], device)

    step_g = {
        b: [hand_on(b, mine[b], 0, 1), hand_on(b, mine[b], 1, 0), hand_on(b, members(b)[1][1], 2, 0)] for b in order
    }

    def core_copy(b, q):
        return remote(ag.at[b, c, q], ag.at[b, c, q], c_s.at[b, q], c_r.at[b, q], core)

    for b in order:
        for i in (0, 2):
            landed(rb.at[b, i], b_r.at[b, i])
        block = s[b, c, mine[b]] + rb[b, 0] + rb[b, 2]
        swapped = jnp.concatenate([swap_virtuals(block[:, i : i + 128], virt) for i in range(0, cols, 128)], axis=1)
        ag[b, c, mine[b]] = factor[b] * (2.0 * block - swapped)
        for copy in step_g[b][:2]:
            copy.start()
        core_copy(b, mine[b]).start()

    for b in order:
        q2 = members(b)[1][1]
        landed(ag.at[b, c, q2], g_r.at[b, 0])
        step_g[b][2].start()
        core_copy(b, q2).start()

    def sent(k, _):
        for copy in send_copies(k):
            copy.wait_send()
        return 0

    lax.fori_loop(count * PARTS - WINDOW, count * PARTS, sent, 0)
    for copy in info_copies:
        copy.wait_send()

    def forward(b):
        (_, q1, _), _, (_, q3, _) = members(b)
        for q, i in ((q1, 1), (q3, 2)):
            landed(ag.at[b, c, q], g_r.at[b, i])
            core_copy(b, q).start()

    def whole(b):
        for q in range(4):
            landed(ag.at[b, 1 - c, q], c_r.at[b, q])
        return ag[b].reshape(cols, cols)

    left, right = pl.ds(0, cols), pl.ds(cols, cols)

    def give_copies(k):
        return (
            remote(rbuf.at[0, place(k)], z.at[Y, place(k)], r_s.at[0, k], r_r.at[0, k], (partner, a)),
            remote(rbuf.at[1, place(k)], z.at[T, place(k)], r_s.at[1, k], r_r.at[1, k], (xd, a)),
            remote(rbuf.at[2, place(k)], z.at[D, place(k)], r_s.at[2, k], r_r.at[2, k], (xt, a)),
        )

    def give_y(k):
        rbuf[0, place(k)] = dot3(beside(held(OWN, k), held(T, k)), (mbh[...], mbl[...]), PLAIN)
        give_copies(k)[0].start()

    def give_t(k):
        rbuf[1, place(k)] = dot3(beside(held(OWN, k), held(Y, k)), (mah[...], mal[...]), TURNED)
        give_copies(k)[1].start()

    def give_d(k):
        rbuf[2, place(k)] = dot3(held(OWN_D, k), (mdh[...], mdl[...]), PLAIN)
        give_copies(k)[2].start()

    for b in (3, 2, 1):
        forward(b)
    t_to_y, own_to_y = whole(3), whole(2)

    @pl.when(yl == 0)
    def _():
        mah[:, right], mal[:, right] = split(t_to_y)
        mbh[right, :], mbl[right, :] = split(t_to_y)
        mbh[left, :], mbl[left, :] = split(own_to_y)

    @pl.when(yl == 1)
    def _():
        turned = t_to_y.T
        mah[:, right], mal[:, right] = split(turned)
        mbh[right, :], mbl[right, :] = split(turned)
        mbh[left, :], mbl[left, :] = split(own_to_y.T)

    give_y(0)
    mah[:, left], mal[:, left] = split(whole(1))
    give_t(0)
    forward(0)
    mdh[...], mdl[...] = split(whole(0))
    give_d(0)

    def finish(k, _):
        @pl.when((k > 0) & (k < count))
        def _():
            @pl.when(k >= WINDOW)
            def _():
                for copy in give_copies(k - WINDOW):
                    copy.wait_send()

            give_y(k)
            give_t(k)
            give_d(k)

        @pl.when(k < count)
        def _():
            y, t, d = (held(block, k) for block in arrivals)
            out_ref[source(side_t, k)] = dot3(t, (mah[:, left], mal[:, left]), PLAIN) + dot3(
                y, (mbh[left, :], mbl[left, :]), TURNED
            )
            out_ref[source(side_d, k)] = dot3(d, (mdh[...], mdl[...]), TURNED)

        @pl.when(k >= LAG)
        def _():
            j = k - LAG
            for i, block in enumerate(arrivals):
                landed(z.at[block, place(j)], r_r.at[i, j])
            out_ref[source(side_t, j)] += z[T, place(j)]
            out_ref[source(side_d, j)] += z[Y, place(j)] + z[D, place(j)]

        return 0

    lax.fori_loop(0, count + LAG, finish, 0)

    def given(k, _):
        for copy in give_copies(k):
            copy.wait_send()
        return 0

    lax.fori_loop(count - WINDOW, count, given, 0)
    for b in order:
        for copy in step_b[b] + [step_next[b]] + step_g[b]:
            copy.wait_send()
        for q in range(4):
            core_copy(b, q).wait_send()


def solution(mesh):
    n_occ = mesh.shape["occ"]

    def shards(three_centre, occ_energy, virt_energy, pair_kept):
        rows, cols = three_centre.shape
        half, chunk = rows // 2, rows // 16
        count = half // chunk
        piece = (cols // 8, cols)
        f32, bf16 = jnp.float32, jnp.bfloat16
        dma = pltpu.SemaphoreType.DMA
        return pl.pallas_call(
            functools.partial(kernel, n_occ, chunk),
            out_shape=pltpu.VMEM((rows, cols), f32),
            in_specs=[pl.BlockSpec(memory_space=pltpu.SMEM)] * 3 + [pl.BlockSpec(memory_space=pl.ANY)],
            out_specs=pl.BlockSpec(memory_space=pltpu.VMEM),
            scratch_shapes=[
                pltpu.VMEM((3, half, cols), f32),
                pltpu.VMEM((5, half, cols), bf16),
                pltpu.VMEM((5, half, cols), bf16),
                pltpu.VMEM((4, 2, 4) + piece, f32),
                pltpu.VMEM((4, 4) + piece, f32),
                pltpu.VMEM((4, 3) + piece, f32),
                pltpu.VMEM((4, 2, 4) + piece, f32),
                pltpu.VMEM((cols, cols), bf16),
                pltpu.VMEM((cols, cols), bf16),
                pltpu.VMEM((cols, 2 * cols), bf16),
                pltpu.VMEM((cols, 2 * cols), bf16),
                pltpu.VMEM((2 * cols, cols), bf16),
                pltpu.VMEM((2 * cols, cols), bf16),
                pltpu.VMEM((3, half, cols), f32),
                pltpu.VMEM((4, 8, cols), f32),
                pltpu.VMEM((4,) + piece, f32),
                dma((3,)), dma((3,)),
                dma((3, count * PARTS)), dma((3, count * PARTS)), dma((2,)),
                dma((4,)), dma((4,)),
                dma((4, 3)), dma((4, 3)),
                dma((4, 3)), dma((4, 3)),
                dma((4, 4)), dma((4, 4)),
                dma((3, count)), dma((3, count)),
            ],
            compiler_params=pltpu.CompilerParams(
                collective_id=0, has_side_effects=True, vmem_limit_bytes=54 * 2**20
            ),
        )(occ_energy, virt_energy, pair_kept.reshape(-1), three_centre)

    return jax.shard_map(
        shards,
        mesh=mesh,
        in_specs=(P("aux", "occ"), P("occ"), P(), P(None, "occ")),
        out_specs=P("aux", "occ"),
        check_vma=False,
    )
```

```python
import functools

import jax
import jax.numpy as jnp
from jax import lax
from jax.experimental import pallas as pl
from jax.experimental.pallas import tpu as pltpu
from jax.sharding import PartitionSpec as P

MESH = pl.DeviceIdType.MESH
Y, T, D, OWN, OWN_D = range(5)
PARTS = 1
WINDOW = 2
LAG = 2


def split(x):
    high = x.astype(jnp.bfloat16)
    return high, (x - high.astype(jnp.float32)).astype(jnp.bfloat16)


def deep_left(*blocks):
    return jnp.concatenate([b[0] for b in blocks] * 2 + [b[1] for b in blocks], axis=1)


def deep_right(*blocks):
    high, low = [b[0] for b in blocks], [b[1] for b in blocks]
    return jnp.concatenate(high + low + high, axis=0)


def product(left, right):
    return jnp.dot(left, right, preferred_element_type=jnp.float32)


def beside(a, b):
    return tuple(jnp.concatenate([x, y], axis=1) for x, y in zip(a, b))


def swap_virtuals(x, virt):
    rows, lanes = x.shape
    row = lax.broadcasted_iota(jnp.int32, x.shape, 0)
    lane = lax.broadcasted_iota(jnp.int32, x.shape, 1)
    step = 1
    while step < virt:
        row_bit, lane_bit = (row & step) != 0, (lane & step) != 0
        from_above = pltpu.roll(pltpu.roll(x, step, 0), lanes - step, 1)
        from_below = pltpu.roll(pltpu.roll(x, rows - step, 0), step, 1)
        moved = jnp.where(row_bit, from_above, from_below)
        x = jnp.where(row_bit == lane_bit, x, moved)
        step *= 2
    return x


def kernel(
    n_occ, chunk,
    occ_ref, virt_ref, kept_ref, b_ref, out_ref,
    z, zhi, zlo, s, ra, rb, ag, kry, krt, kgt, krd, kgd, rbuf, infos, factor,
    info_s, info_r, f_s, f_r, l_s, a_s, a_r, b_s, b_r, g_s, g_r, c_s, c_r, r_s, r_r,
):
    rows, cols = b_ref.shape
    half = rows // 2
    count = half // chunk
    piece = cols // 8
    occ, virt = occ_ref.shape[0], virt_ref.shape[0]

    o, a = lax.axis_index("occ"), lax.axis_index("aux")
    yl, c, yh = lax.rem(o, 2), lax.rem(a, 2), lax.div(a, 2)
    ol, m2 = 1 - yl, o - lax.rem(o, 2)
    up, down = lax.rem(m2 + 2, n_occ), lax.rem(m2 + n_occ - 2, n_occ)
    toward, away = ol * up + yl * down, ol * down + yl * up
    core = (o, a + 1 - 2 * c)
    here, there = a, 2 * (1 - yh) + c
    xd, xt, partner, diagonal = toward + yl, away + yl, m2 + ol, toward + ol
    others = (xt, xd, partner, diagonal)
    tile_there = (1, 0, 2, 3)
    site = (0, 1, yl, yl)

    barrier = pltpu.get_barrier_semaphore()
    everyone = [core, (o, there)] + [(x, y) for x in others for y in (here, there)]
    for device in everyone:
        pl.semaphore_signal(barrier, inc=1, device_id=device, device_id_type=MESH)

    def remote(src, dst, ss, rs, device):
        return pltpu.make_async_remote_copy(
            src_ref=src, dst_ref=dst, send_sem=ss, recv_sem=rs, device_id=device, device_id_type=MESH
        )

    def landed(dst, rs):
        remote(dst, dst, rs, rs, (partner, a)).wait_recv()

    def place(k):
        return pl.ds(pl.multiple_of(k * chunk, chunk), chunk)

    def source(side, k):
        return pl.ds(pl.multiple_of(side * half + k * chunk, chunk), chunk)

    side_t, side_d = ol, yl

    part = chunk // PARTS

    def part_place(k):
        return pl.ds(pl.multiple_of(k * part, part), part)

    def send_copies(k):
        own_t = b_ref.at[pl.ds(pl.multiple_of(side_t * half + k * part, part), part)]
        own_d = b_ref.at[pl.ds(pl.multiple_of(side_d * half + k * part, part), part)]
        return (
            remote(own_d, z.at[Y, part_place(k)], f_s.at[0, k], f_r.at[0, k], (partner, a)),
            remote(own_t, z.at[T, part_place(k)], f_s.at[1, k], f_r.at[1, k], (xt, a)),
            remote(own_d, z.at[D, part_place(k)], f_s.at[2, k], f_r.at[2, k], (xd, a)),
        )

    arrivals = (Y, T, D)
    own = [
        pltpu.make_async_copy(b_ref.at[pl.ds(side_t * half, half)], out_ref.at[pl.ds(side_t * half, half)], l_s.at[0]),
        pltpu.make_async_copy(b_ref.at[pl.ds(side_d * half, half)], out_ref.at[pl.ds(side_d * half, half)], l_s.at[1]),
    ]
    for copy in own:
        copy.start()

    row = lax.broadcasted_iota(jnp.int32, (8, cols), 0)
    lane = lax.broadcasted_iota(jnp.int32, (8, cols), 1)
    levels = jnp.zeros((8, cols), jnp.float32)
    for i in range(occ):
        levels = jnp.where((lane >= i * virt) & (lane < (i + 1) * virt), occ_ref[i], levels)
    empty = jnp.zeros((8, cols), jnp.float32)
    for i in range(virt):
        empty = jnp.where((lane & (virt - 1)) == i, virt_ref[i], empty)
    kept = jnp.where(row == 1, kept_ref[0].astype(jnp.float32), kept_ref[1].astype(jnp.float32))
    infos[0] = jnp.where(row == 0, levels - empty, kept)
    info_copies = [
        remote(infos.at[0], infos.at[i], info_s.at[i - 1], info_r.at[i - 1], (device, a))
        for i, device in ((1, partner), (2, xt), (3, xd))
    ]

    pl.semaphore_wait(barrier, len(everyone))
    for k in range(WINDOW):
        for copy in send_copies(k):
            copy.start()
    for copy in info_copies:
        copy.start()

    def clear(i, _):
        s[i] = jnp.zeros(s.shape[1:], jnp.float32)
        return 0

    lax.fori_loop(0, 4, clear, 0)

    for i in range(3):
        landed(infos.at[i + 1], info_r.at[i])
    mine = [2 * site[b] + yh for b in range(4)]
    row_info, col_info = (0, 2, yl, 2 - yl), (3, 0, ol, 1 + yl)
    kept_info, distance = (3 * yl, 2 * ol, ol, 2 - yl), (2, 2, 1, 1)
    row = lax.broadcasted_iota(jnp.int32, (piece, cols), 0)
    lane = lax.broadcasted_iota(jnp.int32, (piece, cols), 1)
    for b in range(4):
        first = (c * 4 + mine[b]) * piece
        level = jnp.sum(jnp.where(lane == row + first, infos[row_info[b], pl.ds(0, 1)], 0.0), axis=1, keepdims=True)
        gap = level + infos[col_info[b], pl.ds(0, 1)]
        factor[b] = infos[kept_info[b], pl.ds(distance[b], 1)] / gap
    for copy in own:
        copy.wait()

    def add_pair(index, value):
        s[index] += value.reshape(2, 4, piece, cols)

    def held(block, k):
        return zhi[block, place(k)], zlo[block, place(k)]

    def divide(block, k):
        zhi[block, place(k)], zlo[block, place(k)] = split(out_ref[source(side_t if block == OWN else side_d, k)])

    def arrive(k):
        divide(OWN, k)
        divide(OWN_D, k)
        for step in range(PARTS):
            j = k * PARTS + step
            for i, block in enumerate(arrivals):
                landed(z.at[block, part_place(j)], f_r.at[i, j])

            @pl.when(j + WINDOW < count * PARTS)
            def _():
                for copy in send_copies(j):
                    copy.wait_send()
                for copy in send_copies(j + WINDOW):
                    copy.start()

            for block in arrivals:
                zhi[block, part_place(j)], zlo[block, part_place(j)] = split(z[block, part_place(j)])

    def turned(value):
        return deep_left(split(value.T))

    def pairs_t(k):
        right = deep_right(beside(held(OWN, k), held(Y + yl, k)))
        found = product(turned(z[T - yl, place(k)]), right)
        add_pair(1 + yl, found[:, :cols])
        add_pair(3, found[:, cols:])

    def pairs_own(k):
        left = jnp.where(yl == 0, out_ref[source(side_t, k)], z[T, place(k)])
        add_pair(2 - yl, product(turned(left), deep_right(held(ol * Y + yl * OWN, k))))

    def pairs_d(k):
        add_pair(0, product(turned(out_ref[source(side_d, k)]), deep_right(held(D, k))))

    def fetch(k, _):
        arrive(k)
        pairs_t(k)
        pairs_own(k)
        pairs_d(k)
        return 0

    lax.fori_loop(0, count - 1, fetch, 0)

    order = (3, 2, 1, 0)

    def to_core(b):
        return remote(s.at[b, 1 - c], ra.at[b], a_s.at[b], a_r.at[b], core)

    def members(b):
        far = ((o, there), 2 * site[b] + 1 - yh, b)
        same = ((others[b], here), 2 * (1 - site[b]) + yh, tile_there[b])
        other = ((others[b], there), 2 * (1 - site[b]) + 1 - yh, tile_there[b])
        return ((same, far, other), (same, far, other), (same, other, far), (other, same, far))[b]

    step_b, step_next = {}, {}
    for b in order:
        (p1, q1, t1), (p2, q2, t2), (_, q3, _) = members(b)
        step_b[b] = [
            remote(s.at[b, c, q3], rb.at[t1, 1], b_s.at[b, 1], b_r.at[t1, 1], p1),
            remote(s.at[b, c, q1], rb.at[t1, 0], b_s.at[b, 0], b_r.at[t1, 0], p1),
        ]
        step_next[b] = remote(s.at[b, c, q2], rb.at[t2, 2], b_s.at[b, 2], b_r.at[t2, 2], p2)

    def halve(b):
        to_core(b).wait()
        s[b, c] += ra[b]
        for copy in step_b[b]:
            copy.start()

    arrive(count - 1)
    pairs_t(count - 1)
    to_core(3).start()
    to_core(1 + yl).start()
    pairs_own(count - 1)
    to_core(2 - yl).start()
    halve(3)
    pairs_d(count - 1)
    to_core(0).start()
    for b in (2, 1, 0):
        halve(b)
    for b in order:
        q2 = members(b)[1][1]
        landed(rb.at[b, 1], b_r.at[b, 1])
        s[b, c, q2] += rb[b, 1]
        step_next[b].start()

    def hand_on(b, q, i, to):
        device, _, t = members(b)[to]
        return remote(ag.at[b, c, q], ag.at[t, c, q], g_s.at[b, i], g_r.at[t, i], device)

    step_g = {
        b: [hand_on(b, mine[b], 0, 1), hand_on(b, mine[b], 1, 0), hand_on(b, members(b)[1][1], 2, 0)] for b in order
    }

    def core_copy(b, q):
        return remote(ag.at[b, c, q], ag.at[b, c, q], c_s.at[b, q], c_r.at[b, q], core)

    for b in order:
        for i in (0, 2):
            landed(rb.at[b, i], b_r.at[b, i])
        block = s[b, c, mine[b]] + rb[b, 0] + rb[b, 2]
        swapped = jnp.concatenate([swap_virtuals(block[:, i : i + 128], virt) for i in range(0, cols, 128)], axis=1)
        ag[b, c, mine[b]] = factor[b] * (2.0 * block - swapped)
        for copy in step_g[b][:2]:
            copy.start()
        core_copy(b, mine[b]).start()

    for b in order:
        q2 = members(b)[1][1]
        landed(ag.at[b, c, q2], g_r.at[b, 0])
        step_g[b][2].start()
        core_copy(b, q2).start()

    def sent(k, _):
        for copy in send_copies(k):
            copy.wait_send()
        return 0

    lax.fori_loop(count * PARTS - WINDOW, count * PARTS, sent, 0)
    for copy in info_copies:
        copy.wait_send()

    def forward(b):
        (_, q1, _), _, (_, q3, _) = members(b)
        for q, i in ((q1, 1), (q3, 2)):
            landed(ag.at[b, c, q], g_r.at[b, i])
            core_copy(b, q).start()

    def whole(b):
        for q in range(4):
            landed(ag.at[b, 1 - c, q], c_r.at[b, q])
        return ag[b].reshape(cols, cols)

    def put(ref, i, value):
        high, low = split(value)
        n = ref.shape[0] // (3 * cols)
        ref[pl.ds(i * cols, cols), :] = high
        ref[pl.ds((n + i) * cols, cols), :] = low
        ref[pl.ds((2 * n + i) * cols, cols), :] = high

    def give_copies(k):
        return (
            remote(rbuf.at[0, place(k)], z.at[Y, place(k)], r_s.at[0, k], r_r.at[0, k], (partner, a)),
            remote(rbuf.at[1, place(k)], z.at[T, place(k)], r_s.at[1, k], r_r.at[1, k], (xd, a)),
            remote(rbuf.at[2, place(k)], z.at[D, place(k)], r_s.at[2, k], r_r.at[2, k], (xt, a)),
        )

    def give_y(k):
        rbuf[0, place(k)] = product(deep_left(held(OWN, k), held(T, k)), kry[...])
        give_copies(k)[0].start()

    def give_t(k):
        rbuf[1, place(k)] = product(deep_left(held(OWN, k), held(Y, k)), krt[...])
        give_copies(k)[1].start()

    def give_d(k):
        rbuf[2, place(k)] = product(deep_left(held(OWN_D, k)), krd[...])
        give_copies(k)[2].start()

    def both_ways(b):
        value = whole(b)
        other = value.T
        return jnp.where(yl == 0, value, other), jnp.where(yl == 0, other, value)

    for b in (3, 2, 1):
        forward(b)
    t_to_y, y_to_t = both_ways(3)
    put(kry, 1, t_to_y)
    put(krt, 1, y_to_t)
    own_to_y, y_to_own = both_ways(2)
    put(kry, 0, own_to_y)
    give_y(0)
    put(kgt, 1, y_to_own)
    t_to_own = whole(1)
    put(krt, 0, t_to_own.T)
    give_t(0)
    put(kgt, 0, t_to_own)
    forward(0)
    own_to_d = whole(0)
    put(krd, 0, own_to_d)
    give_d(0)
    put(kgd, 0, own_to_d.T)

    def finish(k, _):
        @pl.when((k > 0) & (k < count))
        def _():
            @pl.when(k >= WINDOW)
            def _():
                for copy in give_copies(k - WINDOW):
                    copy.wait_send()

            give_y(k)
            give_t(k)
            give_d(k)

        @pl.when(k < count)
        def _():
            out_ref[source(side_t, k)] = product(deep_left(held(T, k), held(Y, k)), kgt[...])
            out_ref[source(side_d, k)] = product(deep_left(held(D, k)), kgd[...])

        @pl.when(k >= LAG)
        def _():
            j = k - LAG
            for i, block in enumerate(arrivals):
                landed(z.at[block, place(j)], r_r.at[i, j])
            out_ref[source(side_t, j)] += z[T, place(j)]
            out_ref[source(side_d, j)] += z[Y, place(j)] + z[D, place(j)]

        return 0

    lax.fori_loop(0, count + LAG, finish, 0)

    def given(k, _):
        for copy in give_copies(k):
            copy.wait_send()
        return 0

    lax.fori_loop(count - WINDOW, count, given, 0)
    for b in order:
        for copy in step_b[b] + [step_next[b]] + step_g[b]:
            copy.wait_send()
        for q in range(4):
            core_copy(b, q).wait_send()


def solution(mesh):
    n_occ = mesh.shape["occ"]

    def shards(three_centre, occ_energy, virt_energy, pair_kept):
        rows, cols = three_centre.shape
        half, chunk = rows // 2, rows // 16
        count = half // chunk
        piece = (cols // 8, cols)
        f32, bf16 = jnp.float32, jnp.bfloat16
        dma = pltpu.SemaphoreType.DMA
        return pl.pallas_call(
            functools.partial(kernel, n_occ, chunk),
            out_shape=pltpu.VMEM((rows, cols), f32),
            in_specs=[pl.BlockSpec(memory_space=pltpu.SMEM)] * 3 + [pl.BlockSpec(memory_space=pl.ANY)],
            out_specs=pl.BlockSpec(memory_space=pltpu.VMEM),
            scratch_shapes=[
                pltpu.VMEM((3, half, cols), f32),
                pltpu.VMEM((5, half, cols), bf16),
                pltpu.VMEM((5, half, cols), bf16),
                pltpu.VMEM((4, 2, 4) + piece, f32),
                pltpu.VMEM((4, 4) + piece, f32),
                pltpu.VMEM((4, 3) + piece, f32),
                pltpu.VMEM((4, 2, 4) + piece, f32),
                pltpu.VMEM((6 * cols, cols), bf16),
                pltpu.VMEM((6 * cols, cols), bf16),
                pltpu.VMEM((6 * cols, cols), bf16),
                pltpu.VMEM((3 * cols, cols), bf16),
                pltpu.VMEM((3 * cols, cols), bf16),
                pltpu.VMEM((3, half, cols), f32),
                pltpu.VMEM((4, 8, cols), f32),
                pltpu.VMEM((4,) + piece, f32),
                dma((3,)), dma((3,)),
                dma((3, count * PARTS)), dma((3, count * PARTS)), dma((2,)),
                dma((4,)), dma((4,)),
                dma((4, 3)), dma((4, 3)),
                dma((4, 3)), dma((4, 3)),
                dma((4, 4)), dma((4, 4)),
                dma((3, count)), dma((3, count)),
            ],
            compiler_params=pltpu.CompilerParams(
                collective_id=0, has_side_effects=True, vmem_limit_bytes=54 * 2**20
            ),
        )(occ_energy, virt_energy, pair_kept.reshape(-1), three_centre)

    return jax.shard_map(
        shards,
        mesh=mesh,
        in_specs=(P("aux", "occ"), P("occ"), P(), P(None, "occ")),
        out_specs=P("aux", "occ"),
        check_vma=False,
    )
```

```python
import functools

import jax
import jax.numpy as jnp
from jax import lax
from jax.experimental import pallas as pl
from jax.experimental.pallas import tpu as pltpu
from jax.sharding import PartitionSpec as P

MESH = pl.DeviceIdType.MESH
Y, T, D, OWN, OWN_D = range(5)


def split(x):
    high = x.astype(jnp.bfloat16)
    return high, (x - high.astype(jnp.float32)).astype(jnp.bfloat16)


def deep_left(*blocks):
    return jnp.concatenate([b[0] for b in blocks] * 2 + [b[1] for b in blocks], axis=1)


def deep_right(*blocks):
    high, low = [b[0] for b in blocks], [b[1] for b in blocks]
    return jnp.concatenate(high + low + high, axis=0)


def product(left, right):
    return jnp.dot(left, right, preferred_element_type=jnp.float32)


def beside(a, b):
    return tuple(jnp.concatenate([x, y], axis=1) for x, y in zip(a, b))


def swap_virtuals(x, virt):
    rows, lanes = x.shape
    row = lax.broadcasted_iota(jnp.int32, x.shape, 0)
    lane = lax.broadcasted_iota(jnp.int32, x.shape, 1)
    step = 1
    while step < virt:
        row_bit, lane_bit = (row & step) != 0, (lane & step) != 0
        from_above = pltpu.roll(pltpu.roll(x, step, 0), lanes - step, 1)
        from_below = pltpu.roll(pltpu.roll(x, rows - step, 0), step, 1)
        moved = jnp.where(row_bit, from_above, from_below)
        x = jnp.where(row_bit == lane_bit, x, moved)
        step *= 2
    return x


def kernel(
    n_occ, chunk,
    occ_ref, virt_ref, kept_ref, b_ref, out_ref,
    z, zhi, zlo, s, ra, rb, ag, kry, krt, kgt, krd, kgd, rbuf, infos, factor,
    info_s, info_r, f_s, f_r, l_s, a_s, a_r, b_s, b_r, g_s, g_r, c_s, c_r, r_s, r_r,
):
    rows, cols = b_ref.shape
    half = rows // 2
    count = half // chunk
    piece = cols // 8
    occ, virt = occ_ref.shape[0], virt_ref.shape[0]

    o, a = lax.axis_index("occ"), lax.axis_index("aux")
    yl, c, yh = lax.rem(o, 2), lax.rem(a, 2), lax.div(a, 2)
    ol, m2 = 1 - yl, o - lax.rem(o, 2)
    up, down = lax.rem(m2 + 2, n_occ), lax.rem(m2 + n_occ - 2, n_occ)
    toward, away = ol * up + yl * down, ol * down + yl * up
    core = (o, a + 1 - 2 * c)
    here, there = a, 2 * (1 - yh) + c
    xd, xt, partner, diagonal = toward + yl, away + yl, m2 + ol, toward + ol
    others = (xt, xd, partner, diagonal)
    tile_there = (1, 0, 2, 3)
    site = (0, 1, yl, yl)

    barrier = pltpu.get_barrier_semaphore()
    everyone = [core, (o, there)] + [(x, y) for x in others for y in (here, there)]
    for device in everyone:
        pl.semaphore_signal(barrier, inc=1, device_id=device, device_id_type=MESH)

    def remote(src, dst, ss, rs, device):
        return pltpu.make_async_remote_copy(
            src_ref=src, dst_ref=dst, send_sem=ss, recv_sem=rs, device_id=device, device_id_type=MESH
        )

    def landed(dst, rs):
        remote(dst, dst, rs, rs, (partner, a)).wait_recv()

    def place(k):
        return pl.ds(pl.multiple_of(k * chunk, chunk), chunk)

    def source(side, k):
        return pl.ds(pl.multiple_of(side * half + k * chunk, chunk), chunk)

    side_t, side_d = ol, yl

    def send_copies(k):
        own_t, own_d = b_ref.at[source(side_t, k)], b_ref.at[source(side_d, k)]
        return (
            remote(own_d, z.at[Y, place(k)], f_s.at[0, k], f_r.at[0, k], (partner, a)),
            remote(own_t, z.at[T, place(k)], f_s.at[1, k], f_r.at[1, k], (xt, a)),
            remote(own_d, z.at[D, place(k)], f_s.at[2, k], f_r.at[2, k], (xd, a)),
        )

    arrivals = (Y, T, D)
    own = [
        pltpu.make_async_copy(b_ref.at[pl.ds(side_t * half, half)], out_ref.at[pl.ds(side_t * half, half)], l_s.at[0]),
        pltpu.make_async_copy(b_ref.at[pl.ds(side_d * half, half)], out_ref.at[pl.ds(side_d * half, half)], l_s.at[1]),
    ]
    for copy in own:
        copy.start()

    row = lax.broadcasted_iota(jnp.int32, (8, cols), 0)
    lane = lax.broadcasted_iota(jnp.int32, (8, cols), 1)
    levels = jnp.zeros((8, cols), jnp.float32)
    for i in range(occ):
        levels = jnp.where((lane >= i * virt) & (lane < (i + 1) * virt), occ_ref[i], levels)
    empty = jnp.zeros((8, cols), jnp.float32)
    for i in range(virt):
        empty = jnp.where((lane & (virt - 1)) == i, virt_ref[i], empty)
    kept = jnp.where(row == 1, kept_ref[0].astype(jnp.float32), kept_ref[1].astype(jnp.float32))
    infos[0] = jnp.where(row == 0, levels - empty, kept)
    info_copies = [
        remote(infos.at[0], infos.at[i], info_s.at[i - 1], info_r.at[i - 1], (device, a))
        for i, device in ((1, partner), (2, xt), (3, xd))
    ]

    pl.semaphore_wait(barrier, len(everyone))
    for copy in info_copies:
        copy.start()

    def send(k, _):
        for copy in send_copies(k):
            copy.start()
        return 0

    lax.fori_loop(0, count, send, 0)

    def clear(i, _):
        s[i] = jnp.zeros(s.shape[1:], jnp.float32)
        return 0

    lax.fori_loop(0, 4, clear, 0)

    for i in range(3):
        landed(infos.at[i + 1], info_r.at[i])
    mine = [2 * site[b] + yh for b in range(4)]
    row_info, col_info = (0, 2, yl, 2 - yl), (3, 0, ol, 1 + yl)
    kept_info, distance = (3 * yl, 2 * ol, ol, 2 - yl), (2, 2, 1, 1)
    row = lax.broadcasted_iota(jnp.int32, (piece, cols), 0)
    lane = lax.broadcasted_iota(jnp.int32, (piece, cols), 1)
    for b in range(4):
        first = (c * 4 + mine[b]) * piece
        level = jnp.sum(jnp.where(lane == row + first, infos[row_info[b], pl.ds(0, 1)], 0.0), axis=1, keepdims=True)
        gap = level + infos[col_info[b], pl.ds(0, 1)]
        factor[b] = infos[kept_info[b], pl.ds(distance[b], 1)] / gap
    for copy in own:
        copy.wait()

    def add_pair(index, value):
        s[index] += value.reshape(2, 4, piece, cols)

    def held(block, k):
        return zhi[block, place(k)], zlo[block, place(k)]

    def divide(block, k):
        zhi[block, place(k)], zlo[block, place(k)] = split(out_ref[source(side_t if block == OWN else side_d, k)])

    def arrive(k):
        divide(OWN, k)
        divide(OWN_D, k)
        for i, block in enumerate(arrivals):
            landed(z.at[block, place(k)], f_r.at[i, k])
            zhi[block, place(k)], zlo[block, place(k)] = split(z[block, place(k)])

    def turned(value):
        return deep_left(split(value.T))

    def pairs_t(k):
        right = deep_right(beside(held(OWN, k), held(Y + yl, k)))
        found = product(turned(z[T - yl, place(k)]), right)
        add_pair(1 + yl, found[:, :cols])
        add_pair(3, found[:, cols:])

    def pairs_own(k):
        left = jnp.where(yl == 0, out_ref[source(side_t, k)], z[T, place(k)])
        add_pair(2 - yl, product(turned(left), deep_right(held(ol * Y + yl * OWN, k))))

    def pairs_d(k):
        add_pair(0, product(turned(out_ref[source(side_d, k)]), deep_right(held(D, k))))

    def fetch(k, _):
        arrive(k)
        pairs_t(k)
        pairs_own(k)
        pairs_d(k)
        return 0

    lax.fori_loop(0, count - 1, fetch, 0)

    order = (3, 2, 1, 0)

    def to_core(b):
        return remote(s.at[b, 1 - c], ra.at[b], a_s.at[b], a_r.at[b], core)

    def members(b):
        far = ((o, there), 2 * site[b] + 1 - yh, b)
        same = ((others[b], here), 2 * (1 - site[b]) + yh, tile_there[b])
        other = ((others[b], there), 2 * (1 - site[b]) + 1 - yh, tile_there[b])
        return ((same, far, other), (same, far, other), (same, other, far), (other, same, far))[b]

    step_b, step_next = {}, {}
    for b in order:
        (p1, q1, t1), (p2, q2, t2), (_, q3, _) = members(b)
        step_b[b] = [
            remote(s.at[b, c, q3], rb.at[t1, 1], b_s.at[b, 1], b_r.at[t1, 1], p1),
            remote(s.at[b, c, q1], rb.at[t1, 0], b_s.at[b, 0], b_r.at[t1, 0], p1),
        ]
        step_next[b] = remote(s.at[b, c, q2], rb.at[t2, 2], b_s.at[b, 2], b_r.at[t2, 2], p2)

    def halve(b):
        to_core(b).wait()
        s[b, c] += ra[b]
        for copy in step_b[b]:
            copy.start()

    arrive(count - 1)
    pairs_t(count - 1)
    to_core(3).start()
    to_core(1 + yl).start()
    pairs_own(count - 1)
    to_core(2 - yl).start()
    halve(3)
    pairs_d(count - 1)
    to_core(0).start()
    for b in (2, 1, 0):
        halve(b)
    for b in order:
        q2 = members(b)[1][1]
        landed(rb.at[b, 1], b_r.at[b, 1])
        s[b, c, q2] += rb[b, 1]
        step_next[b].start()

    def hand_on(b, q, i, to):
        device, _, t = members(b)[to]
        return remote(ag.at[b, c, q], ag.at[t, c, q], g_s.at[b, i], g_r.at[t, i], device)

    step_g = {
        b: [hand_on(b, mine[b], 0, 1), hand_on(b, mine[b], 1, 0), hand_on(b, members(b)[1][1], 2, 0)] for b in order
    }

    def core_copy(b, q):
        return remote(ag.at[b, c, q], ag.at[b, c, q], c_s.at[b, q], c_r.at[b, q], core)

    for b in order:
        for i in (0, 2):
            landed(rb.at[b, i], b_r.at[b, i])
        block = s[b, c, mine[b]] + rb[b, 0] + rb[b, 2]
        swapped = jnp.concatenate([swap_virtuals(block[:, i : i + 128], virt) for i in range(0, cols, 128)], axis=1)
        ag[b, c, mine[b]] = factor[b] * (2.0 * block - swapped)
        for copy in step_g[b][:2]:
            copy.start()
        core_copy(b, mine[b]).start()

    for b in order:
        q2 = members(b)[1][1]
        landed(ag.at[b, c, q2], g_r.at[b, 0])
        step_g[b][2].start()
        core_copy(b, q2).start()

    def sent(k, _):
        for copy in send_copies(k):
            copy.wait_send()
        return 0

    lax.fori_loop(0, count, sent, 0)
    for copy in info_copies:
        copy.wait_send()

    def forward(b):
        (_, q1, _), _, (_, q3, _) = members(b)
        for q, i in ((q1, 1), (q3, 2)):
            landed(ag.at[b, c, q], g_r.at[b, i])
            core_copy(b, q).start()

    def whole(b):
        for q in range(4):
            landed(ag.at[b, 1 - c, q], c_r.at[b, q])
        return ag[b].reshape(cols, cols)

    def put(ref, i, value):
        high, low = split(value)
        n = ref.shape[0] // (3 * cols)
        ref[pl.ds(i * cols, cols), :] = high
        ref[pl.ds((n + i) * cols, cols), :] = low
        ref[pl.ds((2 * n + i) * cols, cols), :] = high

    def give_copies(k):
        return (
            remote(rbuf.at[0, place(k)], z.at[Y, place(k)], r_s.at[0, k], r_r.at[0, k], (partner, a)),
            remote(rbuf.at[1, place(k)], z.at[T, place(k)], r_s.at[1, k], r_r.at[1, k], (xd, a)),
            remote(rbuf.at[2, place(k)], z.at[D, place(k)], r_s.at[2, k], r_r.at[2, k], (xt, a)),
        )

    def give_y(k):
        rbuf[0, place(k)] = product(deep_left(held(OWN, k), held(T, k)), kry[...])
        give_copies(k)[0].start()

    def give_t(k):
        rbuf[1, place(k)] = product(deep_left(held(OWN, k), held(Y, k)), krt[...])
        give_copies(k)[1].start()

    def give_d(k):
        rbuf[2, place(k)] = product(deep_left(held(OWN_D, k)), krd[...])
        give_copies(k)[2].start()

    def both_ways(b):
        value = whole(b)
        other = value.T
        return jnp.where(yl == 0, value, other), jnp.where(yl == 0, other, value)

    for b in (3, 2, 1):
        forward(b)
    t_to_y, y_to_t = both_ways(3)
    put(kry, 1, t_to_y)
    put(krt, 1, y_to_t)
    own_to_y, y_to_own = both_ways(2)
    put(kry, 0, own_to_y)
    give_y(0)
    put(kgt, 1, y_to_own)
    t_to_own = whole(1)
    put(krt, 0, t_to_own.T)
    give_t(0)
    put(kgt, 0, t_to_own)
    forward(0)
    own_to_d = whole(0)
    put(krd, 0, own_to_d)
    give_d(0)
    put(kgd, 0, own_to_d.T)

    def give(k, _):
        give_y(k)
        give_t(k)
        give_d(k)
        return 0

    lax.fori_loop(1, count, give, 0)

    def finish(k, _):
        found_t = product(deep_left(held(T, k), held(Y, k)), kgt[...])
        found_d = product(deep_left(held(D, k)), kgd[...])
        for i, block in enumerate(arrivals):
            landed(z.at[block, place(k)], r_r.at[i, k])
        out_ref[source(side_t, k)] = found_t + z[T, place(k)]
        out_ref[source(side_d, k)] = found_d + (z[Y, place(k)] + z[D, place(k)])
        return 0

    lax.fori_loop(0, count, finish, 0)

    def given(k, _):
        for copy in give_copies(k):
            copy.wait_send()
        return 0

    lax.fori_loop(0, count, given, 0)
    for b in order:
        for copy in step_b[b] + [step_next[b]] + step_g[b]:
            copy.wait_send()
        for q in range(4):
            core_copy(b, q).wait_send()


def solution(mesh):
    n_occ = mesh.shape["occ"]

    def shards(three_centre, occ_energy, virt_energy, pair_kept):
        rows, cols = three_centre.shape
        half, chunk = rows // 2, rows // 16
        count = half // chunk
        piece = (cols // 8, cols)
        f32, bf16 = jnp.float32, jnp.bfloat16
        dma = pltpu.SemaphoreType.DMA
        return pl.pallas_call(
            functools.partial(kernel, n_occ, chunk),
            out_shape=pltpu.VMEM((rows, cols), f32),
            in_specs=[pl.BlockSpec(memory_space=pltpu.SMEM)] * 3 + [pl.BlockSpec(memory_space=pl.ANY)],
            out_specs=pl.BlockSpec(memory_space=pltpu.VMEM),
            scratch_shapes=[
                pltpu.VMEM((3, half, cols), f32),
                pltpu.VMEM((5, half, cols), bf16),
                pltpu.VMEM((5, half, cols), bf16),
                pltpu.VMEM((4, 2, 4) + piece, f32),
                pltpu.VMEM((4, 4) + piece, f32),
                pltpu.VMEM((4, 3) + piece, f32),
                pltpu.VMEM((4, 2, 4) + piece, f32),
                pltpu.VMEM((6 * cols, cols), bf16),
                pltpu.VMEM((6 * cols, cols), bf16),
                pltpu.VMEM((6 * cols, cols), bf16),
                pltpu.VMEM((3 * cols, cols), bf16),
                pltpu.VMEM((3 * cols, cols), bf16),
                pltpu.VMEM((3, half, cols), f32),
                pltpu.VMEM((4, 8, cols), f32),
                pltpu.VMEM((4,) + piece, f32),
                dma((3,)), dma((3,)),
                dma((3, count)), dma((3, count)), dma((2,)),
                dma((4,)), dma((4,)),
                dma((4, 3)), dma((4, 3)),
                dma((4, 3)), dma((4, 3)),
                dma((4, 4)), dma((4, 4)),
                dma((3, count)), dma((3, count)),
            ],
            compiler_params=pltpu.CompilerParams(
                collective_id=0, has_side_effects=True, vmem_limit_bytes=54 * 2**20
            ),
        )(occ_energy, virt_energy, pair_kept.reshape(-1), three_centre)

    return jax.shard_map(
        shards,
        mesh=mesh,
        in_specs=(P("aux", "occ"), P("occ"), P(), P(None, "occ")),
        out_specs=P("aux", "occ"),
        check_vma=False,
    )
```

```python
import functools

import jax
import jax.numpy as jnp
from jax import lax
from jax.experimental import pallas as pl
from jax.experimental.pallas import tpu as pltpu
from jax.sharding import PartitionSpec as P

MESH = pl.DeviceIdType.MESH
Y, T, D, OWN, OWN_D = range(5)


def split(x):
    high = x.astype(jnp.bfloat16)
    return high, (x - high.astype(jnp.float32)).astype(jnp.bfloat16)


def deep_left(*blocks):
    return jnp.concatenate([b[0] for b in blocks] * 2 + [b[1] for b in blocks], axis=1)


def deep_right(*blocks):
    high, low = [b[0] for b in blocks], [b[1] for b in blocks]
    return jnp.concatenate(high + low + high, axis=0)


def product(left, right):
    return jnp.dot(left, right, preferred_element_type=jnp.float32)


def beside(a, b):
    return tuple(jnp.concatenate([x, y], axis=1) for x, y in zip(a, b))


def swap_virtuals(x, virt):
    rows, lanes = x.shape
    row = lax.broadcasted_iota(jnp.int32, x.shape, 0)
    lane = lax.broadcasted_iota(jnp.int32, x.shape, 1)
    step = 1
    while step < virt:
        row_bit, lane_bit = (row & step) != 0, (lane & step) != 0
        from_above = pltpu.roll(pltpu.roll(x, step, 0), lanes - step, 1)
        from_below = pltpu.roll(pltpu.roll(x, rows - step, 0), step, 1)
        moved = jnp.where(row_bit, from_above, from_below)
        x = jnp.where(row_bit == lane_bit, x, moved)
        step *= 2
    return x


def kernel(
    n_occ, chunk,
    occ_ref, virt_ref, kept_ref, b_ref, out_ref,
    z, zhi, zlo, s, ra, rb, ag, kry, krt, kgt, krd, kgd, rbuf, infos, factor,
    info_s, info_r, f_s, f_r, l_s, a_s, a_r, b_s, b_r, g_s, g_r, c_s, c_r, r_s, r_r,
):
    rows, cols = b_ref.shape
    half = rows // 2
    count = half // chunk
    piece = cols // 8
    occ, virt = occ_ref.shape[0], virt_ref.shape[0]

    o, a = lax.axis_index("occ"), lax.axis_index("aux")
    yl, c, yh = lax.rem(o, 2), lax.rem(a, 2), lax.div(a, 2)
    ol, m2 = 1 - yl, o - lax.rem(o, 2)
    up, down = lax.rem(m2 + 2, n_occ), lax.rem(m2 + n_occ - 2, n_occ)
    toward, away = ol * up + yl * down, ol * down + yl * up
    core = (o, a + 1 - 2 * c)
    here, there = a, 2 * (1 - yh) + c
    xd, xt, partner, diagonal = toward + yl, away + yl, m2 + ol, toward + ol
    others = (xt, xd, partner, diagonal)
    tile_there = (1, 0, 2, 3)
    site = (0, 1, yl, yl)

    barrier = pltpu.get_barrier_semaphore()
    everyone = [core, (o, there)] + [(x, y) for x in others for y in (here, there)]
    for device in everyone:
        pl.semaphore_signal(barrier, inc=1, device_id=device, device_id_type=MESH)

    def remote(src, dst, ss, rs, device):
        return pltpu.make_async_remote_copy(
            src_ref=src, dst_ref=dst, send_sem=ss, recv_sem=rs, device_id=device, device_id_type=MESH
        )

    def landed(dst, rs):
        remote(dst, dst, rs, rs, (partner, a)).wait_recv()

    fine = chunk // 2
    pieces = half // fine

    def place(k, size=chunk):
        return pl.ds(pl.multiple_of(k * size, size), size)

    def source(side, k, size=chunk):
        return pl.ds(pl.multiple_of(side * half + k * size, size), size)

    side_t, side_d = ol, yl

    def send_copies(k):
        own_t, own_d = b_ref.at[source(side_t, k, fine)], b_ref.at[source(side_d, k, fine)]
        return (
            remote(own_d, z.at[Y, place(k, fine)], f_s.at[0, k], f_r.at[0, k], (partner, a)),
            remote(own_t, z.at[T, place(k, fine)], f_s.at[1, k], f_r.at[1, k], (xt, a)),
            remote(own_d, z.at[D, place(k, fine)], f_s.at[2, k], f_r.at[2, k], (xd, a)),
        )

    arrivals = (Y, T, D)
    own = [
        pltpu.make_async_copy(b_ref.at[pl.ds(side_t * half, half)], out_ref.at[pl.ds(side_t * half, half)], l_s.at[0]),
        pltpu.make_async_copy(b_ref.at[pl.ds(side_d * half, half)], out_ref.at[pl.ds(side_d * half, half)], l_s.at[1]),
    ]
    for copy in own:
        copy.start()

    row = lax.broadcasted_iota(jnp.int32, (8, cols), 0)
    lane = lax.broadcasted_iota(jnp.int32, (8, cols), 1)
    levels = jnp.zeros((8, cols), jnp.float32)
    for i in range(occ):
        levels = jnp.where((lane >= i * virt) & (lane < (i + 1) * virt), occ_ref[i], levels)
    empty = jnp.zeros((8, cols), jnp.float32)
    for i in range(virt):
        empty = jnp.where((lane & (virt - 1)) == i, virt_ref[i], empty)
    kept = jnp.where(row == 1, kept_ref[0].astype(jnp.float32), kept_ref[1].astype(jnp.float32))
    infos[0] = jnp.where(row == 0, levels - empty, kept)
    info_copies = [
        remote(infos.at[0], infos.at[i], info_s.at[i - 1], info_r.at[i - 1], (device, a))
        for i, device in ((1, partner), (2, xt), (3, xd))
    ]

    pl.semaphore_wait(barrier, len(everyone))
    for copy in info_copies:
        copy.start()

    def send(k, _):
        for copy in send_copies(k):
            copy.start()
        return 0

    lax.fori_loop(0, pieces, send, 0)

    def clear(i, _):
        s[i] = jnp.zeros(s.shape[1:], jnp.float32)
        return 0

    lax.fori_loop(0, 4, clear, 0)

    for i in range(3):
        landed(infos.at[i + 1], info_r.at[i])
    mine = [2 * site[b] + yh for b in range(4)]
    row_info, col_info = (0, 2, yl, 2 - yl), (3, 0, ol, 1 + yl)
    kept_info, distance = (3 * yl, 2 * ol, ol, 2 - yl), (2, 2, 1, 1)
    row = lax.broadcasted_iota(jnp.int32, (piece, cols), 0)
    lane = lax.broadcasted_iota(jnp.int32, (piece, cols), 1)
    for b in range(4):
        first = (c * 4 + mine[b]) * piece
        level = jnp.sum(jnp.where(lane == row + first, infos[row_info[b], pl.ds(0, 1)], 0.0), axis=1, keepdims=True)
        gap = level + infos[col_info[b], pl.ds(0, 1)]
        factor[b] = infos[kept_info[b], pl.ds(distance[b], 1)] / gap
    for copy in own:
        copy.wait()

    def add_pair(index, value):
        s[index] += value.reshape(2, 4, piece, cols)

    def held(block, k, size=chunk):
        return zhi[block, place(k, size)], zlo[block, place(k, size)]

    def keep(block, k, value):
        zhi[block, place(k, fine)], zlo[block, place(k, fine)] = split(value)

    def arrive(block, k):
        landed(z.at[block, place(k, fine)], f_r.at[block, k])
        keep(block, k, z[block, place(k, fine)])

    def turned(value):
        return deep_left(split(value.T))

    def pairs_t(k):
        right = deep_right(beside(held(OWN, k, fine), held(Y + yl, k, fine)))
        found = product(turned(z[T - yl, place(k, fine)]), right)
        add_pair(1 + yl, found[:, :cols])
        add_pair(3, found[:, cols:])

    def pairs_own(k):
        left = jnp.where(yl == 0, out_ref[source(side_t, k, fine)], z[T, place(k, fine)])
        add_pair(2 - yl, product(turned(left), deep_right(held(ol * Y + yl * OWN, k, fine))))

    def own_parts(k):
        keep(OWN, k, out_ref[source(side_t, k, fine)])
        own_d = out_ref[source(side_d, k, fine)]
        keep(OWN_D, k, own_d)
        return turned(own_d)

    def pairs_d(k, own_d):
        add_pair(0, product(own_d, deep_right(held(D, k, fine))))

    def fetch(k, _):
        own_d = own_parts(k)
        arrive(Y, k)
        arrive(T, k)
        pairs_t(k)
        pairs_own(k)
        arrive(D, k)
        pairs_d(k, own_d)
        return 0

    lax.fori_loop(0, pieces - 1, fetch, 0)

    order = (3, 2, 1, 0)

    def to_core(b):
        return remote(s.at[b, 1 - c], ra.at[b], a_s.at[b], a_r.at[b], core)

    def members(b):
        far = ((o, there), 2 * site[b] + 1 - yh, b)
        same = ((others[b], here), 2 * (1 - site[b]) + yh, tile_there[b])
        other = ((others[b], there), 2 * (1 - site[b]) + 1 - yh, tile_there[b])
        return ((same, far, other), (same, far, other), (same, other, far), (other, same, far))[b]

    step_b, step_next = {}, {}
    for b in order:
        (p1, q1, t1), (p2, q2, t2), (_, q3, _) = members(b)
        step_b[b] = [
            remote(s.at[b, c, q3], rb.at[t1, 1], b_s.at[b, 1], b_r.at[t1, 1], p1),
            remote(s.at[b, c, q1], rb.at[t1, 0], b_s.at[b, 0], b_r.at[t1, 0], p1),
        ]
        step_next[b] = remote(s.at[b, c, q2], rb.at[t2, 2], b_s.at[b, 2], b_r.at[t2, 2], p2)

    def halve(b):
        to_core(b).wait()
        s[b, c] += ra[b]
        for copy in step_b[b]:
            copy.start()

    last = pieces - 1
    own_last = own_parts(last)
    arrive(Y, last)
    arrive(T, last)
    pairs_t(last)
    to_core(3).start()
    to_core(1 + yl).start()
    pairs_own(last)
    to_core(2 - yl).start()
    arrive(D, last)
    pairs_d(last, own_last)
    to_core(0).start()
    halve(3)
    for b in (2, 1, 0):
        halve(b)
    for b in order:
        q2 = members(b)[1][1]
        landed(rb.at[b, 1], b_r.at[b, 1])
        s[b, c, q2] += rb[b, 1]
        step_next[b].start()

    def hand_on(b, q, i, to):
        device, _, t = members(b)[to]
        return remote(ag.at[b, c, q], ag.at[t, c, q], g_s.at[b, i], g_r.at[t, i], device)

    step_g = {
        b: [hand_on(b, mine[b], 0, 1), hand_on(b, mine[b], 1, 0), hand_on(b, members(b)[1][1], 2, 0)] for b in order
    }

    def core_copy(b, q):
        return remote(ag.at[b, c, q], ag.at[b, c, q], c_s.at[b, q], c_r.at[b, q], core)

    for b in order:
        for i in (0, 2):
            landed(rb.at[b, i], b_r.at[b, i])
        block = s[b, c, mine[b]] + rb[b, 0] + rb[b, 2]
        swapped = jnp.concatenate([swap_virtuals(block[:, i : i + 128], virt) for i in range(0, cols, 128)], axis=1)
        ag[b, c, mine[b]] = factor[b] * (2.0 * block - swapped)
        for copy in step_g[b][:2]:
            copy.start()
        core_copy(b, mine[b]).start()

    for b in order:
        q2 = members(b)[1][1]
        landed(ag.at[b, c, q2], g_r.at[b, 0])
        step_g[b][2].start()
        core_copy(b, q2).start()

    def sent(k, _):
        for copy in send_copies(k):
            copy.wait_send()
        return 0

    lax.fori_loop(0, pieces, sent, 0)
    for copy in info_copies:
        copy.wait_send()

    def forward(b):
        (_, q1, _), _, (_, q3, _) = members(b)
        for q, i in ((q1, 1), (q3, 2)):
            landed(ag.at[b, c, q], g_r.at[b, i])
            core_copy(b, q).start()

    def whole(b):
        for q in range(4):
            landed(ag.at[b, 1 - c, q], c_r.at[b, q])
        return ag[b].reshape(cols, cols)

    def put(ref, i, value):
        high, low = split(value)
        n = ref.shape[0] // (3 * cols)
        ref[pl.ds(i * cols, cols), :] = high
        ref[pl.ds((n + i) * cols, cols), :] = low
        ref[pl.ds((2 * n + i) * cols, cols), :] = high

    def give_copies(k):
        return (
            remote(rbuf.at[0, place(k)], z.at[Y, place(k)], r_s.at[0, k], r_r.at[0, k], (partner, a)),
            remote(rbuf.at[1, place(k)], z.at[T, place(k)], r_s.at[1, k], r_r.at[1, k], (xd, a)),
            remote(rbuf.at[2, place(k)], z.at[D, place(k)], r_s.at[2, k], r_r.at[2, k], (xt, a)),
        )

    def give_y(k):
        rbuf[0, place(k)] = product(deep_left(held(OWN, k), held(T, k)), kry[...])
        give_copies(k)[0].start()

    def give_t(k):
        rbuf[1, place(k)] = product(deep_left(held(OWN, k), held(Y, k)), krt[...])
        give_copies(k)[1].start()

    def give_d(k):
        rbuf[2, place(k)] = product(deep_left(held(OWN_D, k)), krd[...])
        give_copies(k)[2].start()

    def both_ways(b):
        value = whole(b)
        other = value.T
        return jnp.where(yl == 0, value, other), jnp.where(yl == 0, other, value)

    for b in (3, 2, 1):
        forward(b)
    t_to_y, y_to_t = both_ways(3)
    put(kry, 1, t_to_y)
    put(krt, 1, y_to_t)
    own_to_y, y_to_own = both_ways(2)
    put(kry, 0, own_to_y)
    give_y(0)
    put(kgt, 1, y_to_own)
    t_to_own = whole(1)
    put(krt, 0, t_to_own.T)
    give_t(0)
    put(kgt, 0, t_to_own)
    forward(0)
    own_to_d = whole(0)
    put(krd, 0, own_to_d)
    give_d(0)
    put(kgd, 0, own_to_d.T)

    def give(k, _):
        give_y(k)
        give_t(k)
        give_d(k)
        return 0

    lax.fori_loop(1, count, give, 0)

    def finish(k, _):
        found_t = product(deep_left(held(T, k), held(Y, k)), kgt[...])
        found_d = product(deep_left(held(D, k)), kgd[...])
        for i, block in enumerate(arrivals):
            landed(z.at[block, place(k)], r_r.at[i, k])
        out_ref[source(side_t, k)] = found_t + z[T, place(k)]
        out_ref[source(side_d, k)] = found_d + (z[Y, place(k)] + z[D, place(k)])
        return 0

    lax.fori_loop(0, count, finish, 0)

    def given(k, _):
        for copy in give_copies(k):
            copy.wait_send()
        return 0

    lax.fori_loop(0, count, given, 0)
    for b in order:
        for copy in step_b[b] + [step_next[b]] + step_g[b]:
            copy.wait_send()
        for q in range(4):
            core_copy(b, q).wait_send()


def solution(mesh):
    n_occ = mesh.shape["occ"]

    def shards(three_centre, occ_energy, virt_energy, pair_kept):
        rows, cols = three_centre.shape
        half, chunk = rows // 2, rows // 16
        count = half // chunk
        piece = (cols // 8, cols)
        f32, bf16 = jnp.float32, jnp.bfloat16
        dma = pltpu.SemaphoreType.DMA
        return pl.pallas_call(
            functools.partial(kernel, n_occ, chunk),
            out_shape=pltpu.VMEM((rows, cols), f32),
            in_specs=[pl.BlockSpec(memory_space=pltpu.SMEM)] * 3 + [pl.BlockSpec(memory_space=pl.ANY)],
            out_specs=pl.BlockSpec(memory_space=pltpu.VMEM),
            scratch_shapes=[
                pltpu.VMEM((3, half, cols), f32),
                pltpu.VMEM((5, half, cols), bf16),
                pltpu.VMEM((5, half, cols), bf16),
                pltpu.VMEM((4, 2, 4) + piece, f32),
                pltpu.VMEM((4, 4) + piece, f32),
                pltpu.VMEM((4, 3) + piece, f32),
                pltpu.VMEM((4, 2, 4) + piece, f32),
                pltpu.VMEM((6 * cols, cols), bf16),
                pltpu.VMEM((6 * cols, cols), bf16),
                pltpu.VMEM((6 * cols, cols), bf16),
                pltpu.VMEM((3 * cols, cols), bf16),
                pltpu.VMEM((3 * cols, cols), bf16),
                pltpu.VMEM((3, half, cols), f32),
                pltpu.VMEM((4, 8, cols), f32),
                pltpu.VMEM((4,) + piece, f32),
                dma((3,)), dma((3,)),
                dma((3, 2 * count)), dma((3, 2 * count)), dma((2,)),
                dma((4,)), dma((4,)),
                dma((4, 3)), dma((4, 3)),
                dma((4, 3)), dma((4, 3)),
                dma((4, 4)), dma((4, 4)),
                dma((3, count)), dma((3, count)),
            ],
            compiler_params=pltpu.CompilerParams(
                collective_id=0, has_side_effects=True, vmem_limit_bytes=54 * 2**20
            ),
        )(occ_energy, virt_energy, pair_kept.reshape(-1), three_centre)

    return jax.shard_map(
        shards,
        mesh=mesh,
        in_specs=(P("aux", "occ"), P("occ"), P(), P(None, "occ")),
        out_specs=P("aux", "occ"),
        check_vma=False,
    )
```

```python
import functools

import jax
import jax.numpy as jnp
from jax import lax
from jax.experimental import pallas as pl
from jax.experimental.pallas import tpu as pltpu
from jax.sharding import PartitionSpec as P

MESH = pl.DeviceIdType.MESH
Y, T, D, OWN, OWN_D = range(5)


def split(x):
    high = x.astype(jnp.bfloat16)
    return high, (x - high.astype(jnp.float32)).astype(jnp.bfloat16)


def deep_left(*blocks):
    return jnp.concatenate([b[0] for b in blocks] * 2 + [b[1] for b in blocks], axis=1)


def deep_right(*blocks):
    high, low = [b[0] for b in blocks], [b[1] for b in blocks]
    return jnp.concatenate(high + low + high, axis=0)


def product(left, right):
    return jnp.dot(left, right, preferred_element_type=jnp.float32)


def beside(a, b):
    return tuple(jnp.concatenate([x, y], axis=1) for x, y in zip(a, b))


def swap_virtuals(x, virt):
    rows, lanes = x.shape
    row = lax.broadcasted_iota(jnp.int32, x.shape, 0)
    lane = lax.broadcasted_iota(jnp.int32, x.shape, 1)
    step = 1
    while step < virt:
        row_bit, lane_bit = (row & step) != 0, (lane & step) != 0
        from_above = pltpu.roll(pltpu.roll(x, step, 0), lanes - step, 1)
        from_below = pltpu.roll(pltpu.roll(x, rows - step, 0), step, 1)
        moved = jnp.where(row_bit, from_above, from_below)
        x = jnp.where(row_bit == lane_bit, x, moved)
        step *= 2
    return x


def kernel(
    n_occ, chunk,
    occ_ref, virt_ref, kept_ref, b_ref, out_ref,
    z, zhi, zlo, s, ra, rb, ag, kry, krt, kgt, krd, kgd, rbuf, infos, factor,
    info_s, info_r, f_s, f_r, l_s, a_s, a_r, b_s, b_r, g_s, g_r, c_s, c_r, r_s, r_r,
):
    rows, cols = b_ref.shape
    half = rows // 2
    count = half // chunk
    piece = cols // 8
    occ, virt = occ_ref.shape[0], virt_ref.shape[0]

    o, a = lax.axis_index("occ"), lax.axis_index("aux")
    yl, c, yh = lax.rem(o, 2), lax.rem(a, 2), lax.div(a, 2)
    ol, m2 = 1 - yl, o - lax.rem(o, 2)
    up, down = lax.rem(m2 + 2, n_occ), lax.rem(m2 + n_occ - 2, n_occ)
    toward, away = ol * up + yl * down, ol * down + yl * up
    core = (o, a + 1 - 2 * c)
    here, there = a, 2 * (1 - yh) + c
    xd, xt, partner, diagonal = toward + yl, away + yl, m2 + ol, toward + ol
    others = (xt, xd, partner, diagonal)
    tile_there = (1, 0, 2, 3)
    site = (0, 1, yl, yl)

    barrier = pltpu.get_barrier_semaphore()
    everyone = [core, (o, there)] + [(x, y) for x in others for y in (here, there)]
    for device in everyone:
        pl.semaphore_signal(barrier, inc=1, device_id=device, device_id_type=MESH)

    def remote(src, dst, ss, rs, device):
        return pltpu.make_async_remote_copy(
            src_ref=src, dst_ref=dst, send_sem=ss, recv_sem=rs, device_id=device, device_id_type=MESH
        )

    def landed(dst, rs):
        remote(dst, dst, rs, rs, (partner, a)).wait_recv()

    fine = chunk // 4
    pieces = half // fine

    def place(k, size=chunk):
        return pl.ds(pl.multiple_of(k * size, size), size)

    def source(side, k, size=chunk):
        return pl.ds(pl.multiple_of(side * half + k * size, size), size)

    side_t, side_d = ol, yl

    def send_copies(k):
        own_t, own_d = b_ref.at[source(side_t, k, fine)], b_ref.at[source(side_d, k, fine)]
        return (
            remote(own_d, z.at[Y, place(k, fine)], f_s.at[0, k], f_r.at[0, k], (partner, a)),
            remote(own_t, z.at[T, place(k, fine)], f_s.at[1, k], f_r.at[1, k], (xt, a)),
            remote(own_d, z.at[D, place(k, fine)], f_s.at[2, k], f_r.at[2, k], (xd, a)),
        )

    arrivals = (Y, T, D)
    own = [
        pltpu.make_async_copy(b_ref.at[pl.ds(side_t * half, half)], out_ref.at[pl.ds(side_t * half, half)], l_s.at[0]),
        pltpu.make_async_copy(b_ref.at[pl.ds(side_d * half, half)], out_ref.at[pl.ds(side_d * half, half)], l_s.at[1]),
    ]
    for copy in own:
        copy.start()

    row = lax.broadcasted_iota(jnp.int32, (8, cols), 0)
    lane = lax.broadcasted_iota(jnp.int32, (8, cols), 1)
    levels = jnp.zeros((8, cols), jnp.float32)
    for i in range(occ):
        levels = jnp.where((lane >= i * virt) & (lane < (i + 1) * virt), occ_ref[i], levels)
    empty = jnp.zeros((8, cols), jnp.float32)
    for i in range(virt):
        empty = jnp.where((lane & (virt - 1)) == i, virt_ref[i], empty)
    kept = jnp.where(row == 1, kept_ref[0].astype(jnp.float32), kept_ref[1].astype(jnp.float32))
    infos[0] = jnp.where(row == 0, levels - empty, kept)
    info_copies = [
        remote(infos.at[0], infos.at[i], info_s.at[i - 1], info_r.at[i - 1], (device, a))
        for i, device in ((1, partner), (2, xt), (3, xd))
    ]

    pl.semaphore_wait(barrier, len(everyone))
    for copy in info_copies:
        copy.start()

    def send(k, _):
        for copy in send_copies(k):
            copy.start()
        return 0

    lax.fori_loop(0, pieces, send, 0)

    def clear(i, _):
        s[i] = jnp.zeros(s.shape[1:], jnp.float32)
        return 0

    lax.fori_loop(0, 4, clear, 0)

    for i in range(3):
        landed(infos.at[i + 1], info_r.at[i])
    mine = [2 * site[b] + yh for b in range(4)]
    row_info, col_info = (0, 2, yl, 2 - yl), (3, 0, ol, 1 + yl)
    kept_info, distance = (3 * yl, 2 * ol, ol, 2 - yl), (2, 2, 1, 1)
    row = lax.broadcasted_iota(jnp.int32, (piece, cols), 0)
    lane = lax.broadcasted_iota(jnp.int32, (piece, cols), 1)
    for b in range(4):
        first = (c * 4 + mine[b]) * piece
        level = jnp.sum(jnp.where(lane == row + first, infos[row_info[b], pl.ds(0, 1)], 0.0), axis=1, keepdims=True)
        gap = level + infos[col_info[b], pl.ds(0, 1)]
        factor[b] = infos[kept_info[b], pl.ds(distance[b], 1)] / gap
    for copy in own:
        copy.wait()

    def add_pair(index, value):
        s[index] += value.reshape(2, 4, piece, cols)

    def held(block, k, size=chunk):
        return zhi[block, place(k, size)], zlo[block, place(k, size)]

    def keep(block, k, value):
        zhi[block, place(k, fine)], zlo[block, place(k, fine)] = split(value)

    def arrive(block, k):
        landed(z.at[block, place(k, fine)], f_r.at[block, k])
        keep(block, k, z[block, place(k, fine)])

    def turned(value):
        return deep_left(split(value.T))

    def pairs_t(k):
        right = deep_right(beside(held(OWN, k, fine), held(Y + yl, k, fine)))
        found = product(turned(z[T - yl, place(k, fine)]), right)
        add_pair(1 + yl, found[:, :cols])
        add_pair(3, found[:, cols:])

    def pairs_own(k):
        left = jnp.where(yl == 0, out_ref[source(side_t, k, fine)], z[T, place(k, fine)])
        add_pair(2 - yl, product(turned(left), deep_right(held(ol * Y + yl * OWN, k, fine))))

    def own_parts(k):
        keep(OWN, k, out_ref[source(side_t, k, fine)])
        own_d = out_ref[source(side_d, k, fine)]
        keep(OWN_D, k, own_d)
        return turned(own_d)

    def pairs_d(k, own_d):
        add_pair(0, product(own_d, deep_right(held(D, k, fine))))

    def fetch(k, _):
        own_d = own_parts(k)
        arrive(Y, k)
        arrive(T, k)
        pairs_t(k)
        pairs_own(k)
        arrive(D, k)
        pairs_d(k, own_d)
        return 0

    lax.fori_loop(0, pieces - 1, fetch, 0)

    order = (3, 2, 1, 0)

    def to_core(b):
        return remote(s.at[b, 1 - c], ra.at[b], a_s.at[b], a_r.at[b], core)

    def members(b):
        far = ((o, there), 2 * site[b] + 1 - yh, b)
        same = ((others[b], here), 2 * (1 - site[b]) + yh, tile_there[b])
        other = ((others[b], there), 2 * (1 - site[b]) + 1 - yh, tile_there[b])
        return ((same, far, other), (same, far, other), (same, other, far), (other, same, far))[b]

    step_b, step_next = {}, {}
    for b in order:
        (p1, q1, t1), (p2, q2, t2), (_, q3, _) = members(b)
        step_b[b] = [
            remote(s.at[b, c, q3], rb.at[t1, 1], b_s.at[b, 1], b_r.at[t1, 1], p1),
            remote(s.at[b, c, q1], rb.at[t1, 0], b_s.at[b, 0], b_r.at[t1, 0], p1),
        ]
        step_next[b] = remote(s.at[b, c, q2], rb.at[t2, 2], b_s.at[b, 2], b_r.at[t2, 2], p2)

    def halve(b):
        to_core(b).wait()
        s[b, c] += ra[b]
        for copy in step_b[b]:
            copy.start()

    last = pieces - 1
    own_last = own_parts(last)
    arrive(Y, last)
    arrive(T, last)
    pairs_t(last)
    to_core(3).start()
    to_core(1 + yl).start()
    pairs_own(last)
    to_core(2 - yl).start()
    arrive(D, last)
    pairs_d(last, own_last)
    to_core(0).start()
    halve(3)
    for b in (2, 1, 0):
        halve(b)
    for b in order:
        q2 = members(b)[1][1]
        landed(rb.at[b, 1], b_r.at[b, 1])
        s[b, c, q2] += rb[b, 1]
        step_next[b].start()

    def hand_on(b, q, i, to):
        device, _, t = members(b)[to]
        return remote(ag.at[b, c, q], ag.at[t, c, q], g_s.at[b, i], g_r.at[t, i], device)

    step_g = {
        b: [hand_on(b, mine[b], 0, 1), hand_on(b, mine[b], 1, 0), hand_on(b, members(b)[1][1], 2, 0)] for b in order
    }

    def core_copy(b, q):
        return remote(ag.at[b, c, q], ag.at[b, c, q], c_s.at[b, q], c_r.at[b, q], core)

    for b in order:
        for i in (0, 2):
            landed(rb.at[b, i], b_r.at[b, i])
        block = s[b, c, mine[b]] + rb[b, 0] + rb[b, 2]
        swapped = jnp.concatenate([swap_virtuals(block[:, i : i + 128], virt) for i in range(0, cols, 128)], axis=1)
        ag[b, c, mine[b]] = factor[b] * (2.0 * block - swapped)
        for copy in step_g[b][:2]:
            copy.start()
        core_copy(b, mine[b]).start()

    for b in order:
        q2 = members(b)[1][1]
        landed(ag.at[b, c, q2], g_r.at[b, 0])
        step_g[b][2].start()
        core_copy(b, q2).start()

    def sent(k, _):
        for copy in send_copies(k):
            copy.wait_send()
        return 0

    lax.fori_loop(0, pieces, sent, 0)
    for copy in info_copies:
        copy.wait_send()

    def forward(b):
        (_, q1, _), _, (_, q3, _) = members(b)
        for q, i in ((q1, 1), (q3, 2)):
            landed(ag.at[b, c, q], g_r.at[b, i])
            core_copy(b, q).start()

    def whole(b):
        for q in range(4):
            landed(ag.at[b, 1 - c, q], c_r.at[b, q])
        return ag[b].reshape(cols, cols)

    def put(ref, i, value):
        high, low = split(value)
        n = ref.shape[0] // (3 * cols)
        ref[pl.ds(i * cols, cols), :] = high
        ref[pl.ds((n + i) * cols, cols), :] = low
        ref[pl.ds((2 * n + i) * cols, cols), :] = high

    def give_copies(k):
        return (
            remote(rbuf.at[0, place(k)], z.at[Y, place(k)], r_s.at[0, k], r_r.at[0, k], (partner, a)),
            remote(rbuf.at[1, place(k)], z.at[T, place(k)], r_s.at[1, k], r_r.at[1, k], (xd, a)),
            remote(rbuf.at[2, place(k)], z.at[D, place(k)], r_s.at[2, k], r_r.at[2, k], (xt, a)),
        )

    def give_y(k):
        rbuf[0, place(k)] = product(deep_left(held(OWN, k), held(T, k)), kry[...])
        give_copies(k)[0].start()

    def give_t(k):
        rbuf[1, place(k)] = product(deep_left(held(OWN, k), held(Y, k)), krt[...])
        give_copies(k)[1].start()

    def give_d(k):
        rbuf[2, place(k)] = product(deep_left(held(OWN_D, k)), krd[...])
        give_copies(k)[2].start()

    def both_ways(b):
        value = whole(b)
        other = value.T
        return jnp.where(yl == 0, value, other), jnp.where(yl == 0, other, value)

    for b in (3, 2, 1):
        forward(b)
    t_to_y, y_to_t = both_ways(3)
    put(kry, 1, t_to_y)
    put(krt, 1, y_to_t)
    own_to_y, y_to_own = both_ways(2)
    put(kry, 0, own_to_y)
    give_y(0)
    put(kgt, 1, y_to_own)
    t_to_own = whole(1)
    put(krt, 0, t_to_own.T)
    give_t(0)
    put(kgt, 0, t_to_own)
    forward(0)
    own_to_d = whole(0)
    put(krd, 0, own_to_d)
    give_d(0)
    put(kgd, 0, own_to_d.T)

    def give(k, _):
        give_y(k)
        give_t(k)
        give_d(k)
        return 0

    lax.fori_loop(1, count, give, 0)

    def finish(k, _):
        found_t = product(deep_left(held(T, k), held(Y, k)), kgt[...])
        found_d = product(deep_left(held(D, k)), kgd[...])
        for i, block in enumerate(arrivals):
            landed(z.at[block, place(k)], r_r.at[i, k])
        out_ref[source(side_t, k)] = found_t + z[T, place(k)]
        out_ref[source(side_d, k)] = found_d + (z[Y, place(k)] + z[D, place(k)])
        return 0

    lax.fori_loop(0, count, finish, 0)

    def given(k, _):
        for copy in give_copies(k):
            copy.wait_send()
        return 0

    lax.fori_loop(0, count, given, 0)
    for b in order:
        for copy in step_b[b] + [step_next[b]] + step_g[b]:
            copy.wait_send()
        for q in range(4):
            core_copy(b, q).wait_send()


def solution(mesh):
    n_occ = mesh.shape["occ"]

    def shards(three_centre, occ_energy, virt_energy, pair_kept):
        rows, cols = three_centre.shape
        half, chunk = rows // 2, rows // 8
        count = half // chunk
        piece = (cols // 8, cols)
        f32, bf16 = jnp.float32, jnp.bfloat16
        dma = pltpu.SemaphoreType.DMA
        return pl.pallas_call(
            functools.partial(kernel, n_occ, chunk),
            out_shape=pltpu.VMEM((rows, cols), f32),
            in_specs=[pl.BlockSpec(memory_space=pltpu.SMEM)] * 3 + [pl.BlockSpec(memory_space=pl.ANY)],
            out_specs=pl.BlockSpec(memory_space=pltpu.VMEM),
            scratch_shapes=[
                pltpu.VMEM((3, half, cols), f32),
                pltpu.VMEM((5, half, cols), bf16),
                pltpu.VMEM((5, half, cols), bf16),
                pltpu.VMEM((4, 2, 4) + piece, f32),
                pltpu.VMEM((4, 4) + piece, f32),
                pltpu.VMEM((4, 3) + piece, f32),
                pltpu.VMEM((4, 2, 4) + piece, f32),
                pltpu.VMEM((6 * cols, cols), bf16),
                pltpu.VMEM((6 * cols, cols), bf16),
                pltpu.VMEM((6 * cols, cols), bf16),
                pltpu.VMEM((3 * cols, cols), bf16),
                pltpu.VMEM((3 * cols, cols), bf16),
                pltpu.VMEM((3, half, cols), f32),
                pltpu.VMEM((4, 8, cols), f32),
                pltpu.VMEM((4,) + piece, f32),
                dma((3,)), dma((3,)),
                dma((3, 4 * count)), dma((3, 4 * count)), dma((2,)),
                dma((4,)), dma((4,)),
                dma((4, 3)), dma((4, 3)),
                dma((4, 3)), dma((4, 3)),
                dma((4, 4)), dma((4, 4)),
                dma((3, count)), dma((3, count)),
            ],
            compiler_params=pltpu.CompilerParams(
                collective_id=0, has_side_effects=True, vmem_limit_bytes=54 * 2**20
            ),
        )(occ_energy, virt_energy, pair_kept.reshape(-1), three_centre)

    return jax.shard_map(
        shards,
        mesh=mesh,
        in_specs=(P("aux", "occ"), P("occ"), P(), P(None, "occ")),
        out_specs=P("aux", "occ"),
        check_vma=False,
    )
```

```python
import functools

import jax
import jax.numpy as jnp
from jax import lax
from jax.experimental import pallas as pl
from jax.experimental.pallas import tpu as pltpu
from jax.sharding import PartitionSpec as P

MESH = pl.DeviceIdType.MESH
Y, T, D, OWN, OWN_D = range(5)


def split(x):
    high = x.astype(jnp.bfloat16)
    return high, (x - high.astype(jnp.float32)).astype(jnp.bfloat16)


def deep_left(*blocks):
    return jnp.concatenate([b[0] for b in blocks] * 2 + [b[1] for b in blocks], axis=1)


def deep_right(*blocks):
    high, low = [b[0] for b in blocks], [b[1] for b in blocks]
    return jnp.concatenate(high + low + high, axis=0)


def product(left, right):
    return jnp.dot(left, right, preferred_element_type=jnp.float32)


def beside(a, b):
    return tuple(jnp.concatenate([x, y], axis=1) for x, y in zip(a, b))


def swap_virtuals(x, virt):
    rows, lanes = x.shape
    row = lax.broadcasted_iota(jnp.int32, x.shape, 0)
    lane = lax.broadcasted_iota(jnp.int32, x.shape, 1)
    step = 1
    while step < virt:
        row_bit, lane_bit = (row & step) != 0, (lane & step) != 0
        from_above = pltpu.roll(pltpu.roll(x, step, 0), lanes - step, 1)
        from_below = pltpu.roll(pltpu.roll(x, rows - step, 0), step, 1)
        moved = jnp.where(row_bit, from_above, from_below)
        x = jnp.where(row_bit == lane_bit, x, moved)
        step *= 2
    return x


def kernel(
    n_occ, chunk,
    occ_ref, virt_ref, kept_ref, b_ref, out_ref,
    z, zhi, zlo, s, ra, rb, ag, kry, krt, kgt, krd, kgd, rbuf, infos, factor,
    info_s, info_r, f_s, f_r, l_s, a_s, a_r, b_s, b_r, g_s, g_r, c_s, c_r, r_s, r_r,
):
    rows, cols = b_ref.shape
    half = rows // 2
    count = half // chunk
    piece = cols // 8
    occ, virt = occ_ref.shape[0], virt_ref.shape[0]

    o, a = lax.axis_index("occ"), lax.axis_index("aux")
    yl, c, yh = lax.rem(o, 2), lax.rem(a, 2), lax.div(a, 2)
    ol, m2 = 1 - yl, o - lax.rem(o, 2)
    up, down = lax.rem(m2 + 2, n_occ), lax.rem(m2 + n_occ - 2, n_occ)
    toward, away = ol * up + yl * down, ol * down + yl * up
    core = (o, a + 1 - 2 * c)
    here, there = a, 2 * (1 - yh) + c
    xd, xt, partner, diagonal = toward + yl, away + yl, m2 + ol, toward + ol
    others = (xt, xd, partner, diagonal)
    tile_there = (1, 0, 2, 3)
    site = (0, 1, yl, yl)

    barrier = pltpu.get_barrier_semaphore()
    everyone = [core, (o, there)] + [(x, y) for x in others for y in (here, there)]
    for device in everyone:
        pl.semaphore_signal(barrier, inc=1, device_id=device, device_id_type=MESH)

    def remote(src, dst, ss, rs, device):
        return pltpu.make_async_remote_copy(
            src_ref=src, dst_ref=dst, send_sem=ss, recv_sem=rs, device_id=device, device_id_type=MESH
        )

    def landed(dst, rs):
        remote(dst, dst, rs, rs, (partner, a)).wait_recv()

    fine = chunk // 2
    pieces = half // fine

    def place(k, size=chunk):
        return pl.ds(pl.multiple_of(k * size, size), size)

    def source(side, k, size=chunk):
        return pl.ds(pl.multiple_of(side * half + k * size, size), size)

    side_t, side_d = ol, yl

    def send_copies(k):
        own_t, own_d = b_ref.at[source(side_t, k, fine)], b_ref.at[source(side_d, k, fine)]
        return (
            remote(own_d, z.at[Y, place(k, fine)], f_s.at[0, k], f_r.at[0, k], (partner, a)),
            remote(own_t, z.at[T, place(k, fine)], f_s.at[1, k], f_r.at[1, k], (xt, a)),
            remote(own_d, z.at[D, place(k, fine)], f_s.at[2, k], f_r.at[2, k], (xd, a)),
        )

    arrivals = (Y, T, D)
    own = [
        pltpu.make_async_copy(b_ref.at[pl.ds(side_t * half, half)], out_ref.at[pl.ds(side_t * half, half)], l_s.at[0]),
        pltpu.make_async_copy(b_ref.at[pl.ds(side_d * half, half)], out_ref.at[pl.ds(side_d * half, half)], l_s.at[1]),
    ]
    for copy in own:
        copy.start()

    row = lax.broadcasted_iota(jnp.int32, (8, cols), 0)
    lane = lax.broadcasted_iota(jnp.int32, (8, cols), 1)
    levels = jnp.zeros((8, cols), jnp.float32)
    for i in range(occ):
        levels = jnp.where((lane >= i * virt) & (lane < (i + 1) * virt), occ_ref[i], levels)
    empty = jnp.zeros((8, cols), jnp.float32)
    for i in range(virt):
        empty = jnp.where((lane & (virt - 1)) == i, virt_ref[i], empty)
    kept = jnp.where(row == 1, kept_ref[0].astype(jnp.float32), kept_ref[1].astype(jnp.float32))
    infos[0] = jnp.where(row == 0, levels - empty, kept)
    info_copies = [
        remote(infos.at[0], infos.at[i], info_s.at[i - 1], info_r.at[i - 1], (device, a))
        for i, device in ((1, partner), (2, xt), (3, xd))
    ]

    pl.semaphore_wait(barrier, len(everyone))
    for copy in info_copies:
        copy.start()

    def send(k, _):
        for copy in send_copies(k):
            copy.start()
        return 0

    lax.fori_loop(0, pieces, send, 0)

    def clear(i, _):
        s[i] = jnp.zeros(s.shape[1:], jnp.float32)
        return 0

    lax.fori_loop(0, 4, clear, 0)

    for i in range(3):
        landed(infos.at[i + 1], info_r.at[i])
    mine = [2 * site[b] + yh for b in range(4)]
    row_info, col_info = (0, 2, yl, 2 - yl), (3, 0, ol, 1 + yl)
    kept_info, distance = (3 * yl, 2 * ol, ol, 2 - yl), (2, 2, 1, 1)
    row = lax.broadcasted_iota(jnp.int32, (piece, cols), 0)
    lane = lax.broadcasted_iota(jnp.int32, (piece, cols), 1)
    for b in range(4):
        first = (c * 4 + mine[b]) * piece
        level = jnp.sum(jnp.where(lane == row + first, infos[row_info[b], pl.ds(0, 1)], 0.0), axis=1, keepdims=True)
        gap = level + infos[col_info[b], pl.ds(0, 1)]
        factor[b] = infos[kept_info[b], pl.ds(distance[b], 1)] / gap
    for copy in own:
        copy.wait()

    def add_pair(index, value):
        s[index] += value.reshape(2, 4, piece, cols)

    def held(block, k, size=chunk):
        return zhi[block, place(k, size)], zlo[block, place(k, size)]

    def keep(block, k, value):
        zhi[block, place(k, fine)], zlo[block, place(k, fine)] = split(value)

    def arrive(block, k):
        landed(z.at[block, place(k, fine)], f_r.at[block, k])
        keep(block, k, z[block, place(k, fine)])

    def turned(value):
        return deep_left(split(value.T))

    def pairs_t(k):
        right = deep_right(beside(held(OWN, k, fine), held(Y + yl, k, fine)))
        found = product(turned(z[T - yl, place(k, fine)]), right)
        add_pair(1 + yl, found[:, :cols])
        add_pair(3, found[:, cols:])

    def pairs_own(k):
        left = jnp.where(yl == 0, out_ref[source(side_t, k, fine)], z[T, place(k, fine)])
        add_pair(2 - yl, product(turned(left), deep_right(held(ol * Y + yl * OWN, k, fine))))

    def own_parts(k):
        keep(OWN, k, out_ref[source(side_t, k, fine)])
        own_d = out_ref[source(side_d, k, fine)]
        keep(OWN_D, k, own_d)
        return turned(own_d)

    def pairs_d(k, own_d):
        add_pair(0, product(own_d, deep_right(held(D, k, fine))))

    def fetch(k, _):
        own_d = own_parts(k)
        arrive(Y, k)
        arrive(T, k)
        pairs_t(k)
        pairs_own(k)
        arrive(D, k)
        pairs_d(k, own_d)
        return 0

    lax.fori_loop(0, pieces - 1, fetch, 0)

    order, later = (0, 1, 2, 3), (2, 1, 0, 3)

    def to_core(b):
        return remote(s.at[b, 1 - c], ra.at[b], a_s.at[b], a_r.at[b], core)

    def members(b):
        far = ((o, there), 2 * site[b] + 1 - yh, b)
        same = ((others[b], here), 2 * (1 - site[b]) + yh, tile_there[b])
        other = ((others[b], there), 2 * (1 - site[b]) + 1 - yh, tile_there[b])
        return ((same, far, other), (same, far, other), (same, other, far), (other, same, far))[b]

    step_b, step_next = {}, {}
    for b in order:
        (p1, q1, t1), (p2, q2, t2), (_, q3, _) = members(b)
        step_b[b] = [
            remote(s.at[b, c, q3], rb.at[t1, 1], b_s.at[b, 1], b_r.at[t1, 1], p1),
            remote(s.at[b, c, q1], rb.at[t1, 0], b_s.at[b, 0], b_r.at[t1, 0], p1),
        ]
        step_next[b] = remote(s.at[b, c, q2], rb.at[t2, 2], b_s.at[b, 2], b_r.at[t2, 2], p2)

    def halve(b):
        to_core(b).wait()
        s[b, c] += ra[b]
        for copy in step_b[b]:
            copy.start()

    last = pieces - 1
    own_last = own_parts(last)
    arrive(D, last)
    pairs_d(last, own_last)
    to_core(0).start()
    arrive(Y, last)
    arrive(T, last)
    pairs_t(last)
    to_core(1 + yl).start()
    to_core(3).start()
    pairs_own(last)
    to_core(2 - yl).start()
    for b in order:
        halve(b)
    for b in order:
        q2 = members(b)[1][1]
        landed(rb.at[b, 1], b_r.at[b, 1])
        s[b, c, q2] += rb[b, 1]
        step_next[b].start()

    def hand_on(b, q, i, to):
        device, _, t = members(b)[to]
        return remote(ag.at[b, c, q], ag.at[t, c, q], g_s.at[b, i], g_r.at[t, i], device)

    step_g = {
        b: [hand_on(b, mine[b], 0, 1), hand_on(b, mine[b], 1, 0), hand_on(b, members(b)[1][1], 2, 0)] for b in order
    }

    def core_copy(b, q):
        return remote(ag.at[b, c, q], ag.at[b, c, q], c_s.at[b, q], c_r.at[b, q], core)

    for b in later:
        for i in (0, 2):
            landed(rb.at[b, i], b_r.at[b, i])
        block = s[b, c, mine[b]] + rb[b, 0] + rb[b, 2]
        swapped = jnp.concatenate([swap_virtuals(block[:, i : i + 128], virt) for i in range(0, cols, 128)], axis=1)
        ag[b, c, mine[b]] = factor[b] * (2.0 * block - swapped)
        for copy in step_g[b][:2]:
            copy.start()
        core_copy(b, mine[b]).start()

    for b in later:
        q2 = members(b)[1][1]
        landed(ag.at[b, c, q2], g_r.at[b, 0])
        step_g[b][2].start()
        core_copy(b, q2).start()

    def sent(k, _):
        for copy in send_copies(k):
            copy.wait_send()
        return 0

    lax.fori_loop(0, pieces, sent, 0)
    for copy in info_copies:
        copy.wait_send()

    def forward(b):
        (_, q1, _), _, (_, q3, _) = members(b)
        for q, i in ((q1, 1), (q3, 2)):
            landed(ag.at[b, c, q], g_r.at[b, i])
            core_copy(b, q).start()

    def whole(b):
        for q in range(4):
            landed(ag.at[b, 1 - c, q], c_r.at[b, q])
        return ag[b].reshape(cols, cols)

    def put(ref, i, value):
        high, low = split(value)
        n = ref.shape[0] // (3 * cols)
        ref[pl.ds(i * cols, cols), :] = high
        ref[pl.ds((n + i) * cols, cols), :] = low
        ref[pl.ds((2 * n + i) * cols, cols), :] = high

    def give_copies(k):
        return (
            remote(rbuf.at[0, place(k)], z.at[Y, place(k)], r_s.at[0, k], r_r.at[0, k], (partner, a)),
            remote(rbuf.at[1, place(k)], z.at[T, place(k)], r_s.at[1, k], r_r.at[1, k], (xd, a)),
            remote(rbuf.at[2, place(k)], z.at[D, place(k)], r_s.at[2, k], r_r.at[2, k], (xt, a)),
        )

    def give_y(k):
        rbuf[0, place(k)] = product(deep_left(held(OWN, k), held(T, k)), kry[...])
        give_copies(k)[0].start()

    def give_t(k):
        rbuf[1, place(k)] = product(deep_left(held(OWN, k), held(Y, k)), krt[...])
        give_copies(k)[1].start()

    def give_d(k):
        rbuf[2, place(k)] = product(deep_left(held(OWN_D, k)), krd[...])
        give_copies(k)[2].start()

    def both_ways(b):
        value = whole(b)
        other = value.T
        return jnp.where(yl == 0, value, other), jnp.where(yl == 0, other, value)

    for b in later:
        forward(b)
    own_to_d = whole(0)
    put(krd, 0, own_to_d)
    give_d(0)
    put(kgd, 0, own_to_d.T)
    t_to_y, y_to_t = both_ways(3)
    put(kry, 1, t_to_y)
    put(krt, 1, y_to_t)
    own_to_y, y_to_own = both_ways(2)
    put(kry, 0, own_to_y)
    give_y(0)
    put(kgt, 1, y_to_own)
    t_to_own = whole(1)
    put(krt, 0, t_to_own.T)
    give_t(0)
    put(kgt, 0, t_to_own)

    def give(k, _):
        give_y(k)
        give_t(k)
        give_d(k)
        return 0

    lax.fori_loop(1, count, give, 0)

    def finish(k, _):
        found_t = product(deep_left(held(T, k), held(Y, k)), kgt[...])
        found_d = product(deep_left(held(D, k)), kgd[...])
        for i, block in enumerate(arrivals):
            landed(z.at[block, place(k)], r_r.at[i, k])
        out_ref[source(side_t, k)] = found_t + z[T, place(k)]
        out_ref[source(side_d, k)] = found_d + (z[Y, place(k)] + z[D, place(k)])
        return 0

    lax.fori_loop(0, count, finish, 0)

    def given(k, _):
        for copy in give_copies(k):
            copy.wait_send()
        return 0

    lax.fori_loop(0, count, given, 0)
    for b in order:
        for copy in step_b[b] + [step_next[b]] + step_g[b]:
            copy.wait_send()
        for q in range(4):
            core_copy(b, q).wait_send()


def solution(mesh):
    n_occ = mesh.shape["occ"]

    def shards(three_centre, occ_energy, virt_energy, pair_kept):
        rows, cols = three_centre.shape
        half, chunk = rows // 2, rows // 16
        count = half // chunk
        piece = (cols // 8, cols)
        f32, bf16 = jnp.float32, jnp.bfloat16
        dma = pltpu.SemaphoreType.DMA
        return pl.pallas_call(
            functools.partial(kernel, n_occ, chunk),
            out_shape=pltpu.VMEM((rows, cols), f32),
            in_specs=[pl.BlockSpec(memory_space=pltpu.SMEM)] * 3 + [pl.BlockSpec(memory_space=pl.ANY)],
            out_specs=pl.BlockSpec(memory_space=pltpu.VMEM),
            scratch_shapes=[
                pltpu.VMEM((3, half, cols), f32),
                pltpu.VMEM((5, half, cols), bf16),
                pltpu.VMEM((5, half, cols), bf16),
                pltpu.VMEM((4, 2, 4) + piece, f32),
                pltpu.VMEM((4, 4) + piece, f32),
                pltpu.VMEM((4, 3) + piece, f32),
                pltpu.VMEM((4, 2, 4) + piece, f32),
                pltpu.VMEM((6 * cols, cols), bf16),
                pltpu.VMEM((6 * cols, cols), bf16),
                pltpu.VMEM((6 * cols, cols), bf16),
                pltpu.VMEM((3 * cols, cols), bf16),
                pltpu.VMEM((3 * cols, cols), bf16),
                pltpu.VMEM((3, half, cols), f32),
                pltpu.VMEM((4, 8, cols), f32),
                pltpu.VMEM((4,) + piece, f32),
                dma((3,)), dma((3,)),
                dma((3, 2 * count)), dma((3, 2 * count)), dma((2,)),
                dma((4,)), dma((4,)),
                dma((4, 3)), dma((4, 3)),
                dma((4, 3)), dma((4, 3)),
                dma((4, 4)), dma((4, 4)),
                dma((3, count)), dma((3, count)),
            ],
            compiler_params=pltpu.CompilerParams(
                collective_id=0, has_side_effects=True, vmem_limit_bytes=54 * 2**20
            ),
        )(occ_energy, virt_energy, pair_kept.reshape(-1), three_centre)

    return jax.shard_map(
        shards,
        mesh=mesh,
        in_specs=(P("aux", "occ"), P("occ"), P(), P(None, "occ")),
        out_specs=P("aux", "occ"),
        check_vma=False,
    )
```

```python
import functools

import jax
import jax.numpy as jnp
from jax import lax
from jax.experimental import pallas as pl
from jax.experimental.pallas import tpu as pltpu
from jax.sharding import PartitionSpec as P

MESH = pl.DeviceIdType.MESH
Y, T, D, OWN, OWN_D = range(5)


def split(x):
    high = x.astype(jnp.bfloat16)
    return high, (x - high.astype(jnp.float32)).astype(jnp.bfloat16)


def deep_left(*blocks):
    return jnp.concatenate([b[0] for b in blocks] * 2 + [b[1] for b in blocks], axis=1)


def deep_right(*blocks):
    high, low = [b[0] for b in blocks], [b[1] for b in blocks]
    return jnp.concatenate(high + low + high, axis=0)


def product(left, right):
    return jnp.dot(left, right, preferred_element_type=jnp.float32)


def beside(a, b):
    return tuple(jnp.concatenate([x, y], axis=1) for x, y in zip(a, b))


def swap_virtuals(x, virt):
    rows, lanes = x.shape
    row = lax.broadcasted_iota(jnp.int32, x.shape, 0)
    lane = lax.broadcasted_iota(jnp.int32, x.shape, 1)
    step = 1
    while step < virt:
        row_bit, lane_bit = (row & step) != 0, (lane & step) != 0
        from_above = pltpu.roll(pltpu.roll(x, step, 0), lanes - step, 1)
        from_below = pltpu.roll(pltpu.roll(x, rows - step, 0), step, 1)
        moved = jnp.where(row_bit, from_above, from_below)
        x = jnp.where(row_bit == lane_bit, x, moved)
        step *= 2
    return x


def kernel(
    n_occ, chunk,
    occ_ref, virt_ref, kept_ref, b_ref, out_ref,
    z, zhi, zlo, s, ra, rb, ag, kry, krt, kgt, krd, kgd, rbuf, infos, factor,
    info_s, info_r, f_s, f_r, l_s, a_s, a_r, b_s, b_r, g_s, g_r, c_s, c_r, r_s, r_r,
):
    rows, cols = b_ref.shape
    half = rows // 2
    count = half // chunk
    piece = cols // 8
    occ, virt = occ_ref.shape[0], virt_ref.shape[0]

    o, a = lax.axis_index("occ"), lax.axis_index("aux")
    yl, c, yh = lax.rem(o, 2), lax.rem(a, 2), lax.div(a, 2)
    ol, m2 = 1 - yl, o - lax.rem(o, 2)
    up, down = lax.rem(m2 + 2, n_occ), lax.rem(m2 + n_occ - 2, n_occ)
    toward, away = ol * up + yl * down, ol * down + yl * up
    core = (o, a + 1 - 2 * c)
    here, there = a, 2 * (1 - yh) + c
    xd, xt, partner, diagonal = toward + yl, away + yl, m2 + ol, toward + ol
    others = (xt, xd, partner, diagonal)
    tile_there = (1, 0, 2, 3)
    site = (0, 1, yl, yl)

    barrier = pltpu.get_barrier_semaphore()
    everyone = [core, (o, there)] + [(x, y) for x in others for y in (here, there)]
    for device in everyone:
        pl.semaphore_signal(barrier, inc=1, device_id=device, device_id_type=MESH)

    def remote(src, dst, ss, rs, device):
        return pltpu.make_async_remote_copy(
            src_ref=src, dst_ref=dst, send_sem=ss, recv_sem=rs, device_id=device, device_id_type=MESH
        )

    def landed(dst, rs):
        remote(dst, dst, rs, rs, (partner, a)).wait_recv()

    fine = chunk // 2
    pieces = half // fine

    def place(k, size=chunk):
        return pl.ds(pl.multiple_of(k * size, size), size)

    def source(side, k, size=chunk):
        return pl.ds(pl.multiple_of(side * half + k * size, size), size)

    side_t, side_d = ol, yl

    def send_copies(k):
        own_t, own_d = b_ref.at[source(side_t, k, fine)], b_ref.at[source(side_d, k, fine)]
        return (
            remote(own_d, z.at[Y, place(k, fine)], f_s.at[0, k], f_r.at[0, k], (partner, a)),
            remote(own_t, z.at[T, place(k, fine)], f_s.at[1, k], f_r.at[1, k], (xt, a)),
            remote(own_d, z.at[D, place(k, fine)], f_s.at[2, k], f_r.at[2, k], (xd, a)),
        )

    arrivals = (Y, T, D)
    own = [
        pltpu.make_async_copy(b_ref.at[pl.ds(side_t * half, half)], out_ref.at[pl.ds(side_t * half, half)], l_s.at[0]),
        pltpu.make_async_copy(b_ref.at[pl.ds(side_d * half, half)], out_ref.at[pl.ds(side_d * half, half)], l_s.at[1]),
    ]
    for copy in own:
        copy.start()

    row = lax.broadcasted_iota(jnp.int32, (8, cols), 0)
    lane = lax.broadcasted_iota(jnp.int32, (8, cols), 1)
    levels = jnp.zeros((8, cols), jnp.float32)
    for i in range(occ):
        levels = jnp.where((lane >= i * virt) & (lane < (i + 1) * virt), occ_ref[i], levels)
    empty = jnp.zeros((8, cols), jnp.float32)
    for i in range(virt):
        empty = jnp.where((lane & (virt - 1)) == i, virt_ref[i], empty)
    kept = jnp.where(row == 1, kept_ref[0].astype(jnp.float32), kept_ref[1].astype(jnp.float32))
    infos[0] = jnp.where(row == 0, levels - empty, kept)
    info_copies = [
        remote(infos.at[0], infos.at[i], info_s.at[i - 1], info_r.at[i - 1], (device, a))
        for i, device in ((1, partner), (2, xt), (3, xd))
    ]

    pl.semaphore_wait(barrier, len(everyone))
    for copy in info_copies:
        copy.start()

    def send(k, _):
        for copy in send_copies(k):
            copy.start()
        return 0

    lax.fori_loop(0, pieces, send, 0)

    def clear(i, _):
        s[i] = jnp.zeros(s.shape[1:], jnp.float32)
        return 0

    lax.fori_loop(0, 4, clear, 0)

    for i in range(3):
        landed(infos.at[i + 1], info_r.at[i])
    mine = [2 * site[b] + yh for b in range(4)]
    row_info, col_info = (0, 2, yl, 2 - yl), (3, 0, ol, 1 + yl)
    kept_info, distance = (3 * yl, 2 * ol, ol, 2 - yl), (2, 2, 1, 1)
    row = lax.broadcasted_iota(jnp.int32, (piece, cols), 0)
    lane = lax.broadcasted_iota(jnp.int32, (piece, cols), 1)
    for b in range(4):
        first = (c * 4 + mine[b]) * piece
        level = jnp.sum(jnp.where(lane == row + first, infos[row_info[b], pl.ds(0, 1)], 0.0), axis=1, keepdims=True)
        gap = level + infos[col_info[b], pl.ds(0, 1)]
        factor[b] = infos[kept_info[b], pl.ds(distance[b], 1)] / gap
    for copy in own:
        copy.wait()

    def add_pair(index, value):
        s[index] += value.reshape(2, 4, piece, cols)

    def held(block, k, size=chunk):
        return zhi[block, place(k, size)], zlo[block, place(k, size)]

    def keep(block, k, value):
        zhi[block, place(k, fine)], zlo[block, place(k, fine)] = split(value)

    def arrive(block, k):
        landed(z.at[block, place(k, fine)], f_r.at[block, k])
        keep(block, k, z[block, place(k, fine)])

    def turned(value):
        return deep_left(split(value.T))

    def pairs_t(k):
        right = deep_right(beside(held(OWN, k, fine), held(Y + yl, k, fine)))
        found = product(turned(z[T - yl, place(k, fine)]), right)
        add_pair(1 + yl, found[:, :cols])
        add_pair(3, found[:, cols:])

    def pairs_own(k):
        left = jnp.where(yl == 0, out_ref[source(side_t, k, fine)], z[T, place(k, fine)])
        add_pair(2 - yl, product(turned(left), deep_right(held(ol * Y + yl * OWN, k, fine))))

    def own_parts(k):
        keep(OWN, k, out_ref[source(side_t, k, fine)])
        own_d = out_ref[source(side_d, k, fine)]
        keep(OWN_D, k, own_d)
        return turned(own_d)

    def pairs_d(k, own_d):
        add_pair(0, product(own_d, deep_right(held(D, k, fine))))

    def fetch(k, _):
        own_d = own_parts(k)
        arrive(Y, k)
        arrive(T, k)
        pairs_t(k)
        pairs_own(k)
        arrive(D, k)
        pairs_d(k, own_d)
        return 0

    lax.fori_loop(0, pieces - 1, fetch, 0)

    order = (3, 2, 1, 0)

    def to_core(b):
        return remote(s.at[b, 1 - c], ra.at[b], a_s.at[b], a_r.at[b], core)

    def members(b):
        far = ((o, there), 2 * site[b] + 1 - yh, b)
        same = ((others[b], here), 2 * (1 - site[b]) + yh, tile_there[b])
        other = ((others[b], there), 2 * (1 - site[b]) + 1 - yh, tile_there[b])
        return ((same, far, other), (same, far, other), (same, other, far), (other, same, far))[b]

    step_b, step_next = {}, {}
    for b in order:
        (p1, q1, t1), (p2, q2, t2), (_, q3, _) = members(b)
        step_b[b] = [
            remote(s.at[b, c, q3], rb.at[t1, 1], b_s.at[b, 1], b_r.at[t1, 1], p1),
            remote(s.at[b, c, q1], rb.at[t1, 0], b_s.at[b, 0], b_r.at[t1, 0], p1),
        ]
        step_next[b] = remote(s.at[b, c, q2], rb.at[t2, 2], b_s.at[b, 2], b_r.at[t2, 2], p2)

    def halve(b):
        to_core(b).wait()
        s[b, c] += ra[b]
        for copy in step_b[b]:
            copy.start()

    last = pieces - 1
    own_last = own_parts(last)
    arrive(Y, last)
    arrive(T, last)
    pairs_t(last)
    to_core(3).start()
    to_core(1 + yl).start()
    pairs_own(last)
    to_core(2 - yl).start()
    arrive(D, last)
    pairs_d(last, own_last)
    to_core(0).start()
    halve(3)
    for b in (2, 1, 0):
        halve(b)
    for b in order:
        q2 = members(b)[1][1]
        landed(rb.at[b, 1], b_r.at[b, 1])
        s[b, c, q2] += rb[b, 1]
        step_next[b].start()

    def hand_on(b, q, i, to):
        device, _, t = members(b)[to]
        return remote(ag.at[b, c, q], ag.at[t, c, q], g_s.at[b, i], g_r.at[t, i], device)

    step_g = {
        b: [hand_on(b, mine[b], 0, 1), hand_on(b, mine[b], 1, 0), hand_on(b, members(b)[1][1], 2, 0)] for b in order
    }

    def core_copy(b, q):
        return remote(ag.at[b, c, q], ag.at[b, c, q], c_s.at[b, q], c_r.at[b, q], core)

    for b in order:
        for i in (0, 2):
            landed(rb.at[b, i], b_r.at[b, i])
        block = s[b, c, mine[b]] + rb[b, 0] + rb[b, 2]
        swapped = jnp.concatenate([swap_virtuals(block[:, i : i + 128], virt) for i in range(0, cols, 128)], axis=1)
        ag[b, c, mine[b]] = factor[b] * (2.0 * block - swapped)
        for copy in step_g[b][:2]:
            copy.start()
        core_copy(b, mine[b]).start()

    for b in order:
        q2 = members(b)[1][1]
        landed(ag.at[b, c, q2], g_r.at[b, 0])
        step_g[b][2].start()
        core_copy(b, q2).start()

    def sent(k, _):
        for copy in send_copies(k):
            copy.wait_send()
        return 0

    lax.fori_loop(0, pieces, sent, 0)
    for copy in info_copies:
        copy.wait_send()

    def forward(b):
        (_, q1, _), _, (_, q3, _) = members(b)
        for q, i in ((q1, 1), (q3, 2)):
            landed(ag.at[b, c, q], g_r.at[b, i])
            core_copy(b, q).start()

    def whole(b):
        for q in range(4):
            landed(ag.at[b, 1 - c, q], c_r.at[b, q])
        return ag[b].reshape(cols, cols)

    def put(ref, i, value):
        high, low = split(value)
        n = ref.shape[0] // (3 * cols)
        ref[pl.ds(i * cols, cols), :] = high
        ref[pl.ds((n + i) * cols, cols), :] = low
        ref[pl.ds((2 * n + i) * cols, cols), :] = high

    def give_copies(k):
        return (
            remote(rbuf.at[0, place(k)], z.at[Y, place(k)], r_s.at[0, k], r_r.at[0, k], (partner, a)),
            remote(rbuf.at[1, place(k)], z.at[T, place(k)], r_s.at[1, k], r_r.at[1, k], (xd, a)),
            remote(rbuf.at[2, place(k)], z.at[D, place(k)], r_s.at[2, k], r_r.at[2, k], (xt, a)),
        )

    def give_y(k):
        rbuf[0, place(k)] = product(deep_left(held(OWN, k), held(T, k)), kry[...])
        give_copies(k)[0].start()

    def give_t(k):
        rbuf[1, place(k)] = product(deep_left(held(OWN, k), held(Y, k)), krt[...])
        give_copies(k)[1].start()

    def give_d(k):
        rbuf[2, place(k)] = product(deep_left(held(OWN_D, k)), krd[...])
        give_copies(k)[2].start()

    def both_ways(b):
        value = whole(b)
        other = value.T
        return jnp.where(yl == 0, value, other), jnp.where(yl == 0, other, value)

    forward(3)
    forward(2)
    t_to_y, y_to_t = both_ways(3)
    put(kry, 1, t_to_y)
    put(krt, 1, y_to_t)
    own_to_y, y_to_own = both_ways(2)
    put(kry, 0, own_to_y)
    give_y(0)
    forward(1)
    put(kgt, 1, y_to_own)
    t_to_own = whole(1)
    put(krt, 0, t_to_own.T)
    give_t(0)
    put(kgt, 0, t_to_own)
    forward(0)
    own_to_d = whole(0)
    put(krd, 0, own_to_d)
    give_d(0)
    put(kgd, 0, own_to_d.T)

    def give(k, _):
        give_y(k)
        give_t(k)
        give_d(k)
        return 0

    lax.fori_loop(1, count, give, 0)

    def finish(k, _):
        found_t = product(deep_left(held(T, k), held(Y, k)), kgt[...])
        found_d = product(deep_left(held(D, k)), kgd[...])
        for i, block in enumerate(arrivals):
            landed(z.at[block, place(k)], r_r.at[i, k])
        out_ref[source(side_t, k)] = found_t + z[T, place(k)]
        out_ref[source(side_d, k)] = found_d + (z[Y, place(k)] + z[D, place(k)])
        return 0

    lax.fori_loop(0, count, finish, 0)

    def given(k, _):
        for copy in give_copies(k):
            copy.wait_send()
        return 0

    lax.fori_loop(0, count, given, 0)
    for b in order:
        for copy in step_b[b] + [step_next[b]] + step_g[b]:
            copy.wait_send()
        for q in range(4):
            core_copy(b, q).wait_send()


def solution(mesh):
    n_occ = mesh.shape["occ"]

    def shards(three_centre, occ_energy, virt_energy, pair_kept):
        rows, cols = three_centre.shape
        half, chunk = rows // 2, rows // 16
        count = half // chunk
        piece = (cols // 8, cols)
        f32, bf16 = jnp.float32, jnp.bfloat16
        dma = pltpu.SemaphoreType.DMA
        return pl.pallas_call(
            functools.partial(kernel, n_occ, chunk),
            out_shape=pltpu.VMEM((rows, cols), f32),
            in_specs=[pl.BlockSpec(memory_space=pltpu.SMEM)] * 3 + [pl.BlockSpec(memory_space=pl.ANY)],
            out_specs=pl.BlockSpec(memory_space=pltpu.VMEM),
            scratch_shapes=[
                pltpu.VMEM((3, half, cols), f32),
                pltpu.VMEM((5, half, cols), bf16),
                pltpu.VMEM((5, half, cols), bf16),
                pltpu.VMEM((4, 2, 4) + piece, f32),
                pltpu.VMEM((4, 4) + piece, f32),
                pltpu.VMEM((4, 3) + piece, f32),
                pltpu.VMEM((4, 2, 4) + piece, f32),
                pltpu.VMEM((6 * cols, cols), bf16),
                pltpu.VMEM((6 * cols, cols), bf16),
                pltpu.VMEM((6 * cols, cols), bf16),
                pltpu.VMEM((3 * cols, cols), bf16),
                pltpu.VMEM((3 * cols, cols), bf16),
                pltpu.VMEM((3, half, cols), f32),
                pltpu.VMEM((4, 8, cols), f32),
                pltpu.VMEM((4,) + piece, f32),
                dma((3,)), dma((3,)),
                dma((3, 2 * count)), dma((3, 2 * count)), dma((2,)),
                dma((4,)), dma((4,)),
                dma((4, 3)), dma((4, 3)),
                dma((4, 3)), dma((4, 3)),
                dma((4, 4)), dma((4, 4)),
                dma((3, count)), dma((3, count)),
            ],
            compiler_params=pltpu.CompilerParams(
                collective_id=0, has_side_effects=True, vmem_limit_bytes=54 * 2**20
            ),
        )(occ_energy, virt_energy, pair_kept.reshape(-1), three_centre)

    return jax.shard_map(
        shards,
        mesh=mesh,
        in_specs=(P("aux", "occ"), P("occ"), P(), P(None, "occ")),
        out_specs=P("aux", "occ"),
        check_vma=False,
    )
```
